256 devices in a mesh: ctx: 32 (over x, y, core), exp: 8 (over z).
Axes of the slice: x: 4, y: 4, z: 8, core: 2. Of those that a mesh axis runs over, the one named last changes fastest.
Arguments:
- queries: bfloat16 [16384, 4096], P('ctx', 'exp'), may hold values from -7 to 7
- key_value_stack: bfloat16 [16384, 2, 512], P('ctx'), may hold values from -6 to 6
- vertical_cols: int32 [128, 4], replicated, may hold values from -1 to 123, as said below
- slash_offsets: int32 [128, 2], replicated, may hold values from 0 to 2, as said below
- resid: bfloat16 [16384, 4096], P(('ctx', 'exp')), may hold values from -6 to 6
- norm_gain: float32 [4096], replicated, may hold values from 0.1 to 1.9
- expert_ids: int32 [16384, 8], P(('ctx', 'exp')), may hold values from 0 to 127, all different within a row; in each aligned block of 64 rows (0 to 63, 64 to 127, ...) at most 5 rows name the same one
- gate_weights: float32 [16384, 8], P(('ctx', 'exp')), may hold values from 0.05 to 1
- w_in: bfloat16 [256, 2048, 1536], P(('ctx', 'exp')), may hold values from -0.09375 to 0.09375
- w_out: bfloat16 [256, 768, 2048], P(('ctx', 'exp')), may hold values from -0.21875 to 0.21875
Outputs:
- mixed: bfloat16 [16384, 4096], P(('ctx', 'exp'))
The draws below stay inside these ranges and needn't reach their ends.
Inputs may be any that keep to these rules, and one draw needn't show every extreme that they name: `vertical_cols`: rows of the first span's query blocks are all -1; every other entry of row i names a block of a span before block i's span (4 blocks a span). The query blocks of one span name at most 2 distinct blocks of any one other span, exactly 2 for some pair of spans. Entries of a row may repeat. slash_offsets[i, 0] is 0 for every query block i. `expert_ids`: in each aligned block of 64 rows no expert is named by more than 5 rows, a bound that some block reaches.
All inputs are finite; a program needn't handle non-finite values.
Results may differ from the reference program's by a relative error of at most 0.006.
Values may be sent and summed in bfloat16 or wider, within the bound.
A program may use at most 128 MiB of HBM per device.

```python
import math
import jax
import jax.numpy as jnp
import numpy as np
from jax import lax

D = 4096
QUERY_HEADS = 32
KEY_VALUE_HEADS = 4
HEAD_SIZE = 128
FF = 768
TOPK = 8
BLOCK_TOKENS = 128
NV = 4
NS = 2
SLASH_REACH = 3
VCAP = 2
SPAN = 512
SEQUENCE_TOKENS = 16384
TOK_DEV = 64
EXPERTS = 128
CAP = 5


def aligned_fields(key, align_rate):
    k_query, random_key_value, k_mark, random_sign_key, k_strength = jax.random.split(key, 5)
    query_vals = jnp.clip(jax.random.normal(k_query, (SEQUENCE_TOKENS, QUERY_HEADS * HEAD_SIZE), jnp.float32), -6.0, 6.0)
    key_value_rows = jnp.clip(jax.random.normal(random_key_value, (SEQUENCE_TOKENS, 2, KEY_VALUE_HEADS * HEAD_SIZE), jnp.float32), -6.0, 6.0)
    places = jnp.arange(SEQUENCE_TOKENS)
    marked_blocks = (jax.random.uniform(k_mark, (SEQUENCE_TOKENS,)) < align_rate) & (places >= 1)
    sign_values = jnp.where(jax.random.uniform(random_sign_key, (SEQUENCE_TOKENS, KEY_VALUE_HEADS, HEAD_SIZE)) < 0.5, -1.0, 1.0)
    signal_strength = 3.0 + 4.0 * jax.random.uniform(k_strength, (SEQUENCE_TOKENS,))
    aligned_rows = jnp.broadcast_to(signal_strength[:, None, None, None] * sign_values[:, :, None, :], (SEQUENCE_TOKENS, KEY_VALUE_HEADS, QUERY_HEADS // KEY_VALUE_HEADS, HEAD_SIZE)).reshape(SEQUENCE_TOKENS, QUERY_HEADS * HEAD_SIZE)
    query_vals = jnp.where(marked_blocks[:, None], aligned_rows, query_vals)
    key_row_slice = key_value_rows[:, 0]
    earlier = jnp.roll(marked_blocks, -1)
    prior_signs = jnp.roll(sign_values, -1, axis=0).reshape(SEQUENCE_TOKENS, KEY_VALUE_HEADS * HEAD_SIZE)
    key_row_slice = jnp.where(earlier[:, None], 3.465 * prior_signs, key_row_slice)
    key_row_slice = jnp.where(marked_blocks[:, None], 3.5 * sign_values.reshape(SEQUENCE_TOKENS, KEY_VALUE_HEADS * HEAD_SIZE), key_row_slice)
    key_value_rows = jnp.stack([key_row_slice, key_value_rows[:, 1]], axis=1)
    return (query_vals, key_value_rows)


def draw_queries(key, part):
    align_rate = 0.0
    query_vals, key_value_rows = aligned_fields(key, align_rate)
    return query_vals.astype(jnp.bfloat16)


def draw_key_value_stack(key, part):
    align_rate = 0.0
    query_vals, key_value_rows = aligned_fields(key, align_rate)
    return key_value_rows.astype(jnp.bfloat16)


def draw_vertical_cols(key, part):
    key = jax.random.fold_in(key, 7)
    k_owner, k_offset, k_pick = jax.random.split(key, 3)
    spans = SEQUENCE_TOKENS // SPAN
    per_span = SPAN // BLOCK_TOKENS
    block_count = SEQUENCE_TOKENS // BLOCK_TOKENS
    home_span = jnp.arange(block_count, dtype=jnp.int32) // per_span
    owners = jax.random.randint(k_owner, (block_count, NV), 0, 1 << 20) % jnp.maximum(home_span, 1)[:, None]
    offset = jax.random.randint(k_offset, (spans, spans), 0, per_span)
    picked = jax.random.randint(k_pick, (block_count, NV), 0, VCAP)
    forced = (jnp.arange(block_count)[:, None] == (spans - 1) * per_span) & (jnp.arange(NV)[None, :] < VCAP)
    owners = jnp.where(forced, 0, owners)
    picked = jnp.where(forced, jnp.arange(NV, dtype=jnp.int32)[None, :], picked)
    start_at = offset[home_span[:, None], owners]
    columns = owners * per_span + (start_at + picked) % per_span
    return jnp.where(home_span[:, None] >= 1, columns, -1).astype(jnp.int32)


def draw_slash_offsets(key, part):
    key = jax.random.fold_in(key, 13)
    block_count = SEQUENCE_TOKENS // BLOCK_TOKENS
    offsets_rest = jax.random.randint(key, (block_count, NS - 1), 1, SLASH_REACH)
    return jnp.concatenate([jnp.zeros((block_count, 1), jnp.int32), offsets_rest], axis=1).astype(jnp.int32)


def level_of(stream_key, dims, pieces, smallest, top_value):
    gain = 1.0
    for axis_at, parts in pieces:
        draws = jax.random.uniform(jax.random.fold_in(jax.random.fold_in(stream_key, 6), axis_at), (parts,), jnp.float32, smallest / len(pieces), top_value / len(pieces))
        gain = gain * jnp.repeat(jnp.exp(draws), dims[axis_at] // parts).reshape((-1,) + (1,) * (len(dims) - 1 - axis_at))
    return gain


def routed_block(own_key, own, number, rows, count, top, reach, lean):
    sequence = jax.random.permutation(own_key, count)
    packed, usual = portions_of(count, rows * top, reach, lean, True), portions_of(count, rows * top, reach, lean, False)
    places = jnp.arange(count)

    def named(tallies, offset_by):
        used = int((tallies > 0).sum())
        fixed = max(1, used // 4)
        passed = fixed + (places - fixed + offset_by * (used - fixed)) % max(1, count - fixed)
        return jnp.zeros((count,), jnp.int32).at[sequence[jnp.where(places < fixed, places, passed)]].set(jnp.asarray(tallies, jnp.int32))

    tallies = jnp.where(number % 4 == 0, named(packed, number // 4), named(usual, number - number // 4 - 1))
    mixed = jax.random.permutation(jax.random.fold_in(own, 3), count)
    donor, receiver = mixed[0:count // 2 * 2:2], mixed[1:count // 2 * 2:2]
    room = jnp.minimum(tallies[donor] - 1, reach - tallies[receiver]) // 2
    room = jnp.where((donor == sequence[0]) | (receiver == sequence[0]) | (tallies[receiver] == 0), 0, jnp.maximum(room, 0))
    passed = jax.random.randint(jax.random.fold_in(own, 4), (count // 2,), 0, 1 << 20) % (room + 1)
    tallies = tallies.at[donor].add(-passed).at[receiver].add(passed)
    items = jnp.searchsorted(jnp.cumsum(tallies), jnp.arange(rows * top), side="right").astype(jnp.int32)
    table = items.reshape(top, rows).T
    table = table[jax.random.permutation(jax.random.fold_in(own, 1), rows)]
    offset_by = jax.random.randint(jax.random.fold_in(own, 2), (rows, 1), 0, top)
    return jnp.take_along_axis(table, (jnp.arange(top)[None, :] + offset_by) % top, axis=1)


def portions_of(count, total, most, slope, full):
    weights = [(1 << 20) // math.isqrt(grade ** slope) + 1 for grade in range(1, count + 1)]
    largest = most if full else min(most, max(-(-total // count), total * weights[0] // sum(weights)))
    least = 1 if total - largest >= count - 1 else 0
    given, rest = [largest] + [least] * (count - 1), total - largest - least * (count - 1)
    while rest > 0:
        free = [i for i in range(1, count) if given[i] < largest] or [i for i in range(1, count) if given[i] < most]
        pool, remaining = sum([weights[i] for i in free]), rest
        for i in free:
            extra = min(most - given[i], max(1, remaining * weights[i] // pool), rest)
            given[i] = given[i] + extra
            rest = rest - extra
    return np.array(given)


def normal_values(stream_key, shape, deviation, bound, cuts=(), kind=jnp.bfloat16):
    factor_of = level_of(stream_key, shape, cuts, -0.22, 0.18) if cuts else 1.0
    values = jax.random.normal(stream_key, shape, jnp.float32) * deviation * factor_of
    return jnp.minimum(jnp.maximum(values, -bound), bound).astype(kind)


def setup_inputs(seed: int = 0) -> dict:
    seeds = jax.random.split(jax.random.key(seed), 11)
    queries = draw_queries(jax.random.fold_in(seeds[10], 71), 0)
    key_value_stack = draw_key_value_stack(jax.random.fold_in(seeds[10], 71), 0)
    vertical_cols = draw_vertical_cols(jax.random.fold_in(seeds[10], 71), 0)
    slash_offsets = draw_slash_offsets(jax.random.fold_in(seeds[10], 71), 0)
    resid = normal_values(seeds[4], (SEQUENCE_TOKENS, D), 1.0, 6.0, ((0, 256),))
    norm_gain = jnp.clip(1.0 + 0.18 * jax.random.normal(seeds[5], (D,), jnp.float32), 0.1, 1.9)
    expert_ids_keys = jax.random.split(jax.random.fold_in(seeds[6], 1), SEQUENCE_TOKENS // TOK_DEV)
    expert_ids_turns = jax.random.permutation(jax.random.fold_in(seeds[6], 3), SEQUENCE_TOKENS // TOK_DEV)
    expert_ids = jax.vmap(lambda own, number: routed_block(jax.random.fold_in(seeds[6], 2), own, number, TOK_DEV, EXPERTS, TOPK, CAP, 1))(expert_ids_keys, expert_ids_turns).reshape((SEQUENCE_TOKENS, TOPK))
    gate_weights = jnp.clip(jnp.exp(math.log(1.0) - 2.9957323 * jax.random.uniform(seeds[7], (SEQUENCE_TOKENS, TOPK), jnp.float32) ** level_of(seeds[7], (SEQUENCE_TOKENS, TOPK), ((0, 256),), -0.2, 0.2)), 0.05, 1.0)
    w_in = normal_values(seeds[8], (2 * EXPERTS, D // 2, 2 * FF), D ** -0.5, 0.09375, ((0, 256),))
    w_out = normal_values(seeds[9], (2 * EXPERTS, FF, D // 2), FF ** -0.5, 0.21875, ((0, 256),))
    return dict(queries=queries, key_value_stack=key_value_stack, vertical_cols=vertical_cols, slash_offsets=slash_offsets, resid=resid, norm_gain=norm_gain, expert_ids=expert_ids, gate_weights=gate_weights, w_in=w_in, w_out=w_out)


def reference(queries, key_value_stack, vertical_cols, slash_offsets, resid, norm_gain, expert_ids, gate_weights, w_in, w_out):
    block_count = SEQUENCE_TOKENS // BLOCK_TOKENS
    query_group_size = QUERY_HEADS // KEY_VALUE_HEADS
    window_width = NS + NV
    key_scale = HEAD_SIZE ** (-0.5)
    key_value_blocks = key_value_stack.reshape(block_count, BLOCK_TOKENS, 2, KEY_VALUE_HEADS, HEAD_SIZE)
    query_block_count = queries.reshape(block_count, BLOCK_TOKENS, KEY_VALUE_HEADS, query_group_size, HEAD_SIZE)
    row_pos = jnp.arange(BLOCK_TOKENS)
    col_pos = jnp.arange(window_width * BLOCK_TOKENS)
    causal = (col_pos[None, :] >= BLOCK_TOKENS) | (col_pos[None, :] <= row_pos[:, None])
    earlier_mask = jnp.arange(NV)[None, :] < jnp.arange(NV)[:, None]

    def attend(block_index):
        slash_ids = block_index - slash_offsets[block_index]
        vertical = vertical_cols[block_index]
        in_slash = jnp.any(vertical[:, None] == slash_ids[None, :], axis=1)
        repeated = jnp.any((vertical[:, None] == vertical[None, :]) & earlier_mask, axis=1)
        usable = jnp.concatenate([slash_ids >= 0, (vertical >= 0) & ~in_slash & ~repeated])
        chosen_block_ids = jnp.maximum(jnp.concatenate([slash_ids, vertical]), 0).astype(jnp.int32)
        chosen_blocks = key_value_blocks[chosen_block_ids].reshape(window_width * BLOCK_TOKENS, 2, KEY_VALUE_HEADS, HEAD_SIZE).astype(jnp.float32)
        query_rows = query_block_count[block_index].astype(jnp.float32)
        scores = jnp.einsum('tgmd,sgd->gmts', query_rows, chosen_blocks[:, 0]) * key_scale
        visible = jnp.repeat(usable, BLOCK_TOKENS)[None, :] & causal
        masked = jnp.where(visible, scores, -1e+30)
        row_max = lax.optimization_barrier(jnp.max(masked, axis=-1, keepdims=True))
        raw_weights = jnp.where(visible, jnp.exp(masked - row_max), 0.0)
        row_sum = lax.optimization_barrier(jnp.sum(raw_weights, axis=-1, keepdims=True))
        probs = (raw_weights / row_sum).astype(jnp.bfloat16)
        result = jnp.einsum('gmts,sgd->tgmd', probs.astype(jnp.float32), chosen_blocks[:, 1])
        return result.astype(jnp.bfloat16).reshape(BLOCK_TOKENS, QUERY_HEADS * HEAD_SIZE)
    attention = lax.map(attend, jnp.arange(block_count, dtype=jnp.int32)).reshape(SEQUENCE_TOKENS, QUERY_HEADS * HEAD_SIZE)
    summed = resid.astype(jnp.float32) + attention.astype(jnp.float32)
    normed = (summed * lax.rsqrt(lax.optimization_barrier(jnp.mean(summed * summed, axis=-1, keepdims=True)) + 1e-06) * norm_gain.astype(jnp.float32)).astype(jnp.bfloat16)
    n_groups = SEQUENCE_TOKENS // TOK_DEV
    per_group = TOK_DEV * TOPK
    flat_ids = expert_ids.reshape(n_groups, per_group)
    onehot = (flat_ids[:, :, None] == jnp.arange(EXPERTS, dtype=jnp.int32)[None, None, :]).astype(jnp.int32)
    before = jnp.cumsum(onehot, axis=1) - onehot
    slots = lax.optimization_barrier(jnp.sum(before * onehot, axis=2))
    token_ids = jnp.broadcast_to(jnp.arange(SEQUENCE_TOKENS, dtype=jnp.int32).reshape(n_groups, TOK_DEV, 1), (n_groups, TOK_DEV, TOPK)).reshape(n_groups, per_group)
    positions = (jnp.arange(n_groups, dtype=jnp.int32)[:, None] * CAP + slots).astype(jnp.int32)
    shares = (gate_weights / lax.optimization_barrier(jnp.sum(gate_weights, axis=1, keepdims=True))).reshape(n_groups, per_group)
    row_table = jnp.full((EXPERTS, n_groups * CAP), SEQUENCE_TOKENS, jnp.int32).at[flat_ids, positions].set(token_ids)
    share_table = jnp.zeros((EXPERTS, n_groups * CAP), jnp.float32).at[flat_ids, positions].set(shares)
    padded = jnp.concatenate([normed, jnp.zeros((1, D), jnp.bfloat16)], axis=0)
    half = D // 2

    def expert_step(expert, combined):
        picks = row_table[expert]
        expert_rows = padded[picks]
        half_low = jnp.dot(expert_rows[:, :half], w_in[2 * expert], preferred_element_type=jnp.float32).astype(jnp.bfloat16)
        half_high = jnp.dot(expert_rows[:, half:], w_in[2 * expert + 1], preferred_element_type=jnp.float32).astype(jnp.bfloat16)
        preact = half_low.astype(jnp.float32) + half_high.astype(jnp.float32)
        hidden = (jax.nn.silu(preact[:, :FF]) * preact[:, FF:]).astype(jnp.bfloat16)
        out_low = jnp.dot(hidden, w_out[2 * expert], preferred_element_type=jnp.float32).astype(jnp.bfloat16)
        out_high = jnp.dot(hidden, w_out[2 * expert + 1], preferred_element_type=jnp.float32).astype(jnp.bfloat16)
        produced = jnp.concatenate([out_low, out_high], axis=1).astype(jnp.float32)
        return combined.at[picks].add(share_table[expert][:, None] * produced)
    combined = lax.fori_loop(0, EXPERTS, expert_step, jnp.zeros((SEQUENCE_TOKENS + 1, D), jnp.float32))
    return (summed + combined[:SEQUENCE_TOKENS]).astype(jnp.bfloat16)
```

```python
import jax
import jax.numpy as jnp
from jax import lax
from jax.experimental import pallas as pl
from jax.experimental.pallas import tpu as pltpu
from jax.sharding import PartitionSpec as P

D = 4096
QUERY_HEADS = 32
KEY_VALUE_HEADS = 4
HEAD_SIZE = 128
FF = 768
TOPK = 8
BLOCK_TOKENS = 128
NV = 4
NS = 2
WINDOW = NS + NV

GRID = 4
CHIPS = GRID * GRID
PLANES = 8
TOK = 64
SPAN = PLANES * TOK
COLUMN = 2 * SPAN
CAP = 5
SLOTS = CAP * 2 * PLANES
GROUP = GRID * SLOTS
ROWS = CHIPS * SLOTS
HALF = D // 2
CHUNKS = 4
CHUNK = HALF // CHUNKS
MESH = pl.DeviceIdType.MESH
BF16 = jnp.bfloat16
F32 = jnp.float32


def attend_kernel(ids, usable, q_ref, *refs):
    kv, o_ref = refs[:WINDOW], refs[WINDOW]
    block = pl.program_id(0)
    heads = q_ref.shape[1] // HEAD_SIZE
    q = jnp.concatenate([q_ref[:, h * HEAD_SIZE : (h + 1) * HEAD_SIZE] for h in range(heads)], axis=0)
    keys = jnp.concatenate([kv[j][0, :, :HEAD_SIZE] for j in range(WINDOW)], axis=0)
    values = jnp.concatenate([kv[j][0, :, HEAD_SIZE:] for j in range(WINDOW)], axis=0)
    scores = lax.dot_general(q, keys, (((1,), (1,)), ((), ())), preferred_element_type=F32)
    scores = scores * HEAD_SIZE ** (-0.5)
    row = lax.broadcasted_iota(jnp.int32, (heads * BLOCK_TOKENS, BLOCK_TOKENS), 0) % BLOCK_TOKENS
    col = lax.broadcasted_iota(jnp.int32, (heads * BLOCK_TOKENS, BLOCK_TOKENS), 1)
    parts, masks = [], []
    for j in range(WINDOW):
        part = scores[:, j * BLOCK_TOKENS : (j + 1) * BLOCK_TOKENS]
        seen = jnp.full(part.shape, usable[block * WINDOW + j], jnp.int32) > 0
        if j == 0:
            seen = seen & (col <= row)
        parts.append(jnp.where(seen, part, -1e30))
        masks.append(seen)
    top = parts[0]
    for part in parts[1:]:
        top = jnp.maximum(top, part)
    top = jnp.max(top, axis=1, keepdims=True)
    parts = [jnp.where(seen, jnp.exp(part - top), 0.0) for part, seen in zip(parts, masks)]
    total = parts[0]
    for part in parts[1:]:
        total = total + part
    total = jnp.sum(total, axis=1, keepdims=True)
    probs = jnp.concatenate([(part / total).astype(BF16) for part in parts], axis=1)
    result = jnp.dot(probs, values, preferred_element_type=F32).astype(BF16)
    for h in range(heads):
        o_ref[:, h * HEAD_SIZE : (h + 1) * HEAD_SIZE] = result[h * BLOCK_TOKENS : (h + 1) * BLOCK_TOKENS]


def attend(queries, kv_blocks, ids, usable):
    blocks = queries.shape[0] // BLOCK_TOKENS
    width = queries.shape[1]

    def kv_spec(j):
        return pl.BlockSpec((1, BLOCK_TOKENS, 2 * HEAD_SIZE), lambda i, ids, usable: (ids[i * WINDOW + j], 0, 0))

    return pl.pallas_call(
        attend_kernel,
        grid_spec=pltpu.PrefetchScalarGridSpec(
            num_scalar_prefetch=2,
            grid=(blocks,),
            in_specs=[pl.BlockSpec((BLOCK_TOKENS, width), lambda i, ids, usable: (i, 0))]
            + [kv_spec(j) for j in range(WINDOW)],
            out_specs=pl.BlockSpec((BLOCK_TOKENS, width), lambda i, ids, usable: (i, 0)),
        ),
        out_shape=jax.ShapeDtypeStruct(queries.shape, BF16),
        compiler_params=pltpu.CompilerParams(vmem_limit_bytes=32 * 2**20),
        name="attend",
    )(ids, usable, queries, *([kv_blocks] * WINDOW))


def expert_kernel(
    attn, resid, gain, pos_in, pos_out, share_out, w_own, w_got, w_out, out,
    heads_in, gath, toks, hot, sent, rows, win, wout, mine, theirs, hid_out, hid, back, comb, sib, parts,
    a_s, a_r, r_s, r_r, l_s, l_r, c_s, c_r, d_s, d_r, p_s, p_r, h_s, h_r, o_s, o_r, u_s, u_r, z_s, z_r, w_s,
):
    ctx = lax.axis_index("ctx")
    z = lax.axis_index("exp")
    chip, c = lax.div(ctx, 2), lax.rem(ctx, 2)
    x, y = lax.div(chip, GRID), lax.rem(chip, GRID)
    sibling = chip * 2 + 1 - c
    mate = lax.div(z, 2) * 2 + 1 - lax.rem(z, 2)
    same = c == lax.rem(z, 2)
    apart = c != lax.rem(z, 2)

    def send(src, dst, s_sem, r_sem, to_ctx, to_z):
        return pltpu.make_async_remote_copy(
            src_ref=src, dst_ref=dst, send_sem=s_sem, recv_sem=r_sem,
            device_id=(to_ctx, to_z), device_id_type=MESH,
        )

    def loop(count, body):
        lax.fori_loop(0, count, lambda i, carry: (body(i), carry)[1], 0)

    def mod8(v):
        return lax.rem(v + 2 * PLANES, PLANES)

    barrier = pltpu.get_barrier_semaphore()

    def greet(cx, zz):
        pl.semaphore_signal(barrier, inc=1, device_id=(cx, zz), device_id_type=MESH)

    def greet_chip(d):
        @pl.when(d != chip)
        def _():
            greet(d * 2 + c, z)

    loop(CHIPS, greet_chip)
    loop(PLANES - 1, lambda r: greet(ctx, mod8(z + r + 1)))
    greet(sibling, z)
    greet(sibling, mate)

    def win_copy(ref, k):
        return pltpu.make_async_copy(ref.at[pl.ds(k * CHUNK, CHUNK), :], win.at[k], w_s.at[k])

    def wout_copy(k):
        return pltpu.make_async_copy(w_out.at[:, pl.ds(k * CHUNK, CHUNK)], wout.at[k], w_s.at[CHUNKS + k])

    for k in range(CHUNKS):
        @pl.when(same)
        def _():
            win_copy(w_own, k).start()

        @pl.when(apart)
        def _():
            win_copy(w_got, k).start()

        wout_copy(k).start()

    pl.semaphore_wait(barrier, (CHIPS - 1) + (PLANES - 1) + 2)

    def a_send(r):
        to = mod8(z + r + 1)
        return send(attn.at[pl.ds(pl.multiple_of(to * TOK, TOK), TOK), :], heads_in.at[z], a_s.at[to], a_r.at[z], ctx, to)

    loop(PLANES - 1, lambda r: a_send(r).start())
    heads_in[z] = attn[pl.ds(pl.multiple_of(z * TOK, TOK), TOK), :]

    def a_wait(r):
        src = mod8(z + r + 1)
        send(heads_in.at[src], heads_in.at[src], a_s.at[src], a_r.at[src], ctx, src).wait_recv()

    loop(PLANES - 1, a_wait)

    squares = jnp.zeros((TOK, 1), F32)
    for b in range(PLANES):
        summed = resid[:, b * CHUNK : (b + 1) * CHUNK].astype(F32) + heads_in[b].astype(F32)
        squares = squares + jnp.sum(summed * summed, axis=1, keepdims=True)
    scale = lax.rsqrt(squares / D + 1e-06)
    for b in range(PLANES):
        summed = resid[:, b * CHUNK : (b + 1) * CHUNK].astype(F32) + heads_in[b].astype(F32)
        gath[b % CHUNKS, z, b // CHUNKS] = (summed * scale * gain[:, b * CHUNK : (b + 1) * CHUNK]).astype(BF16)

    def piece(k, r, slot, half):
        return gath.at[k, slot] if r < 4 else gath.at[k, slot, half]

    def right(k, r):
        ref = piece(k, r, mod8(z - r + 1), 0)
        return send(ref, ref, r_s.at[k, r - 1], r_r.at[k, r - 1], ctx, mod8(z + 1))

    def left(k, r):
        ref = piece(k, r, mod8(z + r - 1), 1)
        return send(ref, ref, l_s.at[k, r - 1], l_r.at[k, r - 1], ctx, mod8(z - 1))

    def right_in(k, r):
        ref = piece(k, r, mod8(z - r), 0)
        return send(ref, ref, r_s.at[k, r - 1], r_r.at[k, r - 1], ctx, mod8(z + 1))

    def left_in(k, r):
        ref = piece(k, r, mod8(z + r), 1)
        return send(ref, ref, l_s.at[k, r - 1], l_r.at[k, r - 1], ctx, mod8(z - 1))

    def place(core, slot):
        return pl.ds(pl.multiple_of(core * SPAN + slot * TOK, TOK), TOK)

    def across(k, slot):
        return send(
            gath.at[k, slot, 1 - c], toks.at[k, place(c, slot), :], c_s.at[k, slot], c_r.at[k, slot], sibling, z
        )

    def across_in(k, slot):
        return send(
            gath.at[k, slot, 1 - c], toks.at[k, place(1 - c, slot), :], c_s.at[k, slot], c_r.at[k, slot], sibling, z
        )

    def arrived(k, slot):
        across(k, slot).start()
        toks[k, place(c, slot), :] = gath[k, slot, c]

    def d_send(k, d):
        at = pl.ds(pl.multiple_of(d * SLOTS, SLOTS), SLOTS)
        to = pl.ds(pl.multiple_of(chip * SLOTS, SLOTS), SLOTS)
        return send(sent.at[k, at, :], rows.at[k, to, :], d_s.at[k, d], d_r.at[k, chip], d * 2 + c, z)

    own = pl.ds(pl.multiple_of(chip * SLOTS, SLOTS), SLOTS)

    def dispatch(k):
        loop(PLANES, lambda s: across_in(k, s).wait_recv())

        def step(g):
            xd = lax.rem(x + g, GRID)
            slot = lax.broadcasted_iota(jnp.int32, (SLOTS, COLUMN), 0)
            for i in range(GRID):
                hot[i * SLOTS : (i + 1) * SLOTS, :] = jnp.where(slot == pos_in[xd * GRID + i], 1.0, 0.0).astype(BF16)
            at = pl.ds(pl.multiple_of(xd * GROUP, GROUP), GROUP)
            sent[k, at, :] = jnp.dot(hot[...], toks[k], preferred_element_type=F32).astype(BF16)
            for j in range(1, GRID):
                d_send(k, xd * GRID + lax.rem(y + j, GRID)).start()

            @pl.when(g > 0)
            def _():
                d_send(k, xd * GRID + y).start()

        loop(GRID, step)
        rows[k, own, :] = sent[k, own, :]

    for tick in range(1, 2 * CHUNKS + 4):
        for k in range(CHUNKS):
            r = tick - 2 * k
            if 2 <= r <= 5:
                right_in(k, r - 1).wait_recv()
                left_in(k, r - 1).wait_recv()
            if 1 <= r <= 4:
                right(k, r).start()
                left(k, r).start()
            if r == 1:
                arrived(k, z)
            if 2 <= r <= 4:
                arrived(k, mod8(z - r + 1))
                arrived(k, mod8(z + r - 1))
            if r == 5:
                arrived(k, mod8(z + 4))
        for k in range(CHUNKS):
            if tick - 2 * k == 5:
                dispatch(k)

    lane = lax.broadcasted_iota(jnp.int32, (HEAD_SIZE, ROWS), 1)
    owner = lax.broadcasted_iota(jnp.int32, (HEAD_SIZE, ROWS), 0) * SLOTS
    spread = jnp.where((lane >= owner) & (lane < owner + SLOTS), 1.0, 0.0).astype(BF16)

    def build(b):
        at = pl.ds(pl.multiple_of(b * 128, 128), 128)
        slot = jnp.dot(pos_out[at, :], spread, preferred_element_type=F32)
        share = jnp.dot(share_out[at, :], spread, preferred_element_type=F32)
        want = lax.rem(lax.broadcasted_iota(jnp.int32, (128, ROWS), 1), SLOTS).astype(F32)
        comb[at, :] = jnp.where(slot == want, share, 0.0).astype(BF16)

    loop(COLUMN // 128, build)

    for k in range(CHUNKS):
        win_copy(w_own, k).wait()
        wout_copy(k).wait()

    def span_of(g):
        xs = lax.rem(x - g + GRID, GRID)
        return xs, pl.ds(pl.multiple_of(xs * GROUP, GROUP), GROUP)

    def p_send(g):
        _, at = span_of(g)
        return send(mine.at[at, :], theirs.at[at, :], p_s.at[g], p_r.at[g], sibling, z)

    def first(g):
        xs, at = span_of(g)
        for i in range(GRID):
            src = xs * GRID + i

            @pl.when(src != chip)
            def _():
                for k in range(CHUNKS):
                    ref = rows.at[k, pl.ds(pl.multiple_of(src * SLOTS, SLOTS), SLOTS), :]
                    send(ref, ref, d_s.at[k, src], d_r.at[k, src], src * 2 + c, z).wait_recv()

        total = jnp.dot(rows[0, at, :], win[0], preferred_element_type=F32)
        for k in range(1, CHUNKS):
            total = total + jnp.dot(rows[k, at, :], win[k], preferred_element_type=F32)
        mine[at, :] = total.astype(BF16)
        p_send(g).start()

    loop(GRID, first)

    def h_send(g):
        _, at = span_of(g)
        return send(hid_out.at[at, :], hid.at[at, :], h_s.at[g], h_r.at[g], sibling, mate)

    def hidden(g):
        p_send(g).wait_recv()
        xs, _ = span_of(g)

        def part(i):
            at = pl.ds(pl.multiple_of(xs * GROUP + i * 32, 32), 32)
            pre = mine[at, :].astype(F32) + theirs[at, :].astype(F32)
            gate, up = pre[:, :FF], pre[:, FF:]
            value = (gate / (1.0 + jnp.exp(-gate)) * up).astype(BF16)

            @pl.when(same)
            def _():
                hid[at, :] = value

            @pl.when(apart)
            def _():
                hid_out[at, :] = value

        loop(GROUP // 32, part)

        @pl.when(apart)
        def _():
            h_send(g).start()

    loop(GRID, hidden)

    def d_done(k):
        def one(d):
            @pl.when(d != chip)
            def _():
                d_send(k, d).wait_send()

        loop(CHIPS, one)

    loop(CHUNKS, d_done)

    def o_send(n, d):
        at = pl.ds(pl.multiple_of(d * SLOTS, SLOTS), SLOTS)
        return send(sent.at[n, at, :], back.at[n, own, :], o_s.at[n, d], o_r.at[n, chip], d * 2 + c, z)

    def second(step):
        n, g = lax.div(step, GRID), lax.rem(step, GRID)
        xs, at = span_of(g)

        @pl.when((n == 0) & apart)
        def _():
            send(hid_out.at[at, :], hid.at[at, :], h_s.at[g], h_r.at[g], sibling, mate).wait_recv()

        sent[n, at, :] = jnp.dot(hid[at, :], wout[n], preferred_element_type=F32).astype(BF16)
        for j in range(1, GRID):
            o_send(n, xs * GRID + lax.rem(y + j, GRID)).start()

        @pl.when(g > 0)
        def _():
            o_send(n, xs * GRID + y).start()

        @pl.when(g == 0)
        def _():
            back[n, own, :] = sent[n, own, :]

    loop(CHUNKS * GRID, second)

    def ring_done(k):
        for r in range(1, 5):
            right(k, r).wait_send()
            left(k, r).wait_send()
        loop(PLANES, lambda s: across(k, s).wait_send())

    loop(CHUNKS, ring_done)

    def u_send(n):
        return send(toks.at[n, pl.ds(0, SPAN), :], sib.at[n], u_s.at[n], u_r.at[n], sibling, z)

    def z_send(n, to):
        return send(gath.at[n, to, 0], parts.at[n, z], z_s.at[n, to], z_r.at[n, z], ctx, to)

    def tokens_of(core):
        return pl.ds(pl.multiple_of(core * SPAN, SPAN), SPAN)

    def combine(step):
        @pl.when(step < CHUNKS)
        def _():
            n = step

            def one(d):
                @pl.when(d != chip)
                def _():
                    ref = back.at[n, pl.ds(pl.multiple_of(d * SLOTS, SLOTS), SLOTS), :]
                    send(ref, ref, o_s.at[n, d], o_r.at[n, d], d * 2 + c, z).wait_recv()

            loop(CHIPS, one)
            toks[n, pl.ds(0, SPAN), :] = jnp.dot(
                comb[tokens_of(1 - c), :], back[n], preferred_element_type=F32
            ).astype(BF16)
            u_send(n).start()

        @pl.when(step > 0)
        def _():
            n = step - 1
            total = jnp.dot(comb[tokens_of(c), :], back[n], preferred_element_type=F32)
            u_send(n).wait_recv()
            total = (total + sib[n].astype(F32)).astype(BF16)
            for s in range(PLANES):
                gath[n, s, 0] = total[s * TOK : (s + 1) * TOK]
            loop(PLANES - 1, lambda r: z_send(n, mod8(z + r + 1)).start())
            parts[n, z] = gath[n, z, 0]

    loop(CHUNKS + 1, combine)

    for n in range(CHUNKS):
        def one(r):
            src = mod8(z + r + 1)
            send(parts.at[n, src], parts.at[n, src], z_s.at[n, src], z_r.at[n, src], ctx, src).wait_recv()

        loop(PLANES - 1, one)
        for half in range(2):
            b = half * CHUNKS + n
            total = parts[n, half].astype(F32)
            for q in range(1, PLANES // 2):
                total = total + parts[n, 2 * q + half].astype(F32)
            summed = resid[:, b * CHUNK : (b + 1) * CHUNK].astype(F32) + heads_in[b].astype(F32)
            out[:, b * CHUNK : (b + 1) * CHUNK] = (summed + total).astype(BF16)

    loop(PLANES - 1, lambda r: a_send(r).wait_send())

    def last(g):
        p_send(g).wait_send()

        @pl.when(apart)
        def _():
            h_send(g).wait_send()

    loop(GRID, last)

    def left_all(n):
        def one(d):
            @pl.when(d != chip)
            def _():
                o_send(n, d).wait_send()

        loop(CHIPS, one)
        u_send(n).wait_send()
        loop(PLANES - 1, lambda r: z_send(n, mod8(z + r + 1)).wait_send())

    loop(CHUNKS, left_all)


def run_experts(attn, resid, gain, pos_in, pos_out, share_out, w_own, w_got, w_out):
    vmem = pl.BlockSpec(memory_space=pltpu.VMEM)
    hbm = pl.BlockSpec(memory_space=pl.ANY)
    dma = pltpu.SemaphoreType.DMA
    return pl.pallas_call(
        expert_kernel,
        out_shape=jax.ShapeDtypeStruct((TOK, D), BF16),
        in_specs=[vmem] * 6 + [hbm] * 3,
        out_specs=vmem,
        scratch_shapes=[
            pltpu.VMEM((PLANES, TOK, CHUNK), BF16),
            pltpu.VMEM((CHUNKS, PLANES, 2, TOK, CHUNK), BF16),
            pltpu.VMEM((CHUNKS, COLUMN, CHUNK), BF16),
            pltpu.VMEM((GROUP, COLUMN), BF16),
            pltpu.VMEM((CHUNKS, ROWS, CHUNK), BF16),
            pltpu.VMEM((CHUNKS, ROWS, CHUNK), BF16),
            pltpu.VMEM((CHUNKS, CHUNK, 2 * FF), BF16),
            pltpu.VMEM((CHUNKS, FF, CHUNK), BF16),
            pltpu.VMEM((ROWS, 2 * FF), BF16),
            pltpu.VMEM((ROWS, 2 * FF), BF16),
            pltpu.VMEM((ROWS, FF), BF16),
            pltpu.VMEM((ROWS, FF), BF16),
            pltpu.VMEM((CHUNKS, ROWS, CHUNK), BF16),
            pltpu.VMEM((COLUMN, ROWS), BF16),
            pltpu.VMEM((CHUNKS, SPAN, CHUNK), BF16),
            pltpu.VMEM((CHUNKS, PLANES, TOK, CHUNK), BF16),
            dma((PLANES,)), dma((PLANES,)),
            dma((CHUNKS, 4)), dma((CHUNKS, 4)),
            dma((CHUNKS, 4)), dma((CHUNKS, 4)),
            dma((CHUNKS, PLANES)), dma((CHUNKS, PLANES)),
            dma((CHUNKS, CHIPS)), dma((CHUNKS, CHIPS)),
            dma((GRID,)), dma((GRID,)),
            dma((GRID,)), dma((GRID,)),
            dma((CHUNKS, CHIPS)), dma((CHUNKS, CHIPS)),
            dma((CHUNKS,)), dma((CHUNKS,)),
            dma((CHUNKS, PLANES)), dma((CHUNKS, PLANES)),
            dma((2 * CHUNKS,)),
        ],
        compiler_params=pltpu.CompilerParams(
            collective_id=0, has_side_effects=True, vmem_limit_bytes=62 * 2**20
        ),
        cost_estimate=pl.CostEstimate(flops=25 * 10**9, bytes_accessed=12 * 10**6, transcendentals=10**6),
        name="experts",
    )(attn, resid, gain, pos_in, pos_out, share_out, w_own, w_got, w_out)


def local(
    queries, key_value_stack, vertical_cols, slash_offsets, resid,
    norm_gain, expert_ids, gate_weights, w_in, w_out,
):
    n_ctx = lax.axis_size("ctx")
    ctx = lax.axis_index("ctx")
    z = lax.axis_index("exp")
    core = ctx % 2
    blocks = queries.shape[0] // BLOCK_TOKENS
    heads_dev = queries.shape[1] // HEAD_SIZE

    kv_head = z * heads_dev // (QUERY_HEADS // KEY_VALUE_HEADS)
    own_kv = lax.dynamic_slice_in_dim(key_value_stack, kv_head * HEAD_SIZE, HEAD_SIZE, 2)
    own_kv = own_kv.reshape(blocks, BLOCK_TOKENS, 2 * HEAD_SIZE)
    kv_blocks = lax.all_gather(own_kv, "ctx", axis=0, tiled=True)

    route = []
    for i in range(n_ctx):
        for j in range(PLANES):
            if i % 2 != j % 2:
                route.append((i * PLANES + j, (i ^ 1) * PLANES + (j ^ 1)))
    w_own = w_in[0]
    w_got = lax.ppermute(w_own, ("ctx", "exp"), route)

    shares = gate_weights / jnp.sum(gate_weights, axis=1, keepdims=True)
    routing = jnp.concatenate([expert_ids.astype(F32), shares], axis=1)
    routing = lax.all_gather(routing, "exp", axis=0, tiled=True)
    other = lax.ppermute(routing, "ctx", [(i, i ^ 1) for i in range(n_ctx)])
    routing = jnp.where(
        core == 0, jnp.concatenate([routing, other], axis=0), jnp.concatenate([other, routing], axis=0)
    )
    ids = routing[:, :TOPK].astype(jnp.int32).T
    named = ids[None, :, :] == (jnp.arange(n_ctx, dtype=jnp.int32) * (PLANES // 2) + z // 2)[:, None, None]
    share = jnp.sum(jnp.where(named, routing[:, TOPK:].T[None], 0.0), axis=1)
    member = jnp.any(named, axis=1)
    upper = (jnp.arange(COLUMN)[:, None] < jnp.arange(COLUMN)[None, :]).astype(BF16)
    rank = jnp.dot(member.astype(BF16), upper, preferred_element_type=F32)
    pos = jnp.where(member, rank, -1.0).reshape(CHIPS, 2, COLUMN)
    share = share.reshape(CHIPS, 2, COLUMN)
    pos_in = lax.dynamic_slice_in_dim(pos, z % 2, 1, 1).astype(jnp.int32)
    pos_out = lax.dynamic_slice_in_dim(pos, core, 1, 1)[:, 0].T
    share_out = lax.dynamic_slice_in_dim(share, core, 1, 1)[:, 0].T
    pad = ((0, 0), (0, HEAD_SIZE - CHIPS))
    pos_out = jnp.pad(pos_out.astype(BF16), pad)
    share_out = jnp.pad(share_out.astype(BF16), pad)

    first = ctx * blocks
    cols = lax.dynamic_slice_in_dim(vertical_cols, first, blocks, 0)
    offsets = lax.dynamic_slice_in_dim(slash_offsets, first, blocks, 0)
    slash = (first + jnp.arange(blocks, dtype=jnp.int32))[:, None] - offsets
    in_slash = jnp.any(cols[:, :, None] == slash[:, None, :], axis=2)
    earlier = jnp.arange(NV)[None, :] < jnp.arange(NV)[:, None]
    repeated = jnp.any((cols[:, :, None] == cols[:, None, :]) & earlier[None], axis=2)
    usable = jnp.concatenate([slash >= 0, (cols >= 0) & ~in_slash & ~repeated], axis=1)
    chosen = jnp.maximum(jnp.concatenate([slash, cols], axis=1), 0)
    attn = attend(queries, kv_blocks, chosen.reshape(-1), usable.astype(jnp.int32).reshape(-1))

    return run_experts(attn, resid, norm_gain[None, :], pos_in, pos_out, share_out, w_own, w_got, w_out[0])


def solution(mesh):
    in_specs = (
        P("ctx", "exp"),
        P("ctx", None, None),
        P(),
        P(),
        P(("ctx", "exp"), None),
        P(),
        P(("ctx", "exp"), None),
        P(("ctx", "exp"), None),
        P(("ctx", "exp"), None, None),
        P(("ctx", "exp"), None, None),
    )
    out_specs = P(("ctx", "exp"), None)
    return jax.shard_map(local, mesh=mesh, in_specs=in_specs, out_specs=out_specs, check_vma=False)
```

```python
import jax
import jax.numpy as jnp
from jax import lax
from jax.experimental import pallas as pl
from jax.experimental.pallas import tpu as pltpu
from jax.sharding import PartitionSpec as P

D = 4096
QUERY_HEADS = 32
KEY_VALUE_HEADS = 4
HEAD_SIZE = 128
FF = 768
TOPK = 8
BLOCK_TOKENS = 128
NV = 4
NS = 2
WINDOW = NS + NV

GRID = 4
CHIPS = GRID * GRID
PLANES = 8
TOK = 64
SPAN = PLANES * TOK
COLUMN = 2 * SPAN
CAP = 5
SLOTS = CAP * 2 * PLANES
GROUP = GRID * SLOTS
ROWS = CHIPS * SLOTS
HALF = D // 2
CHUNKS = 8
CHUNK = HALF // CHUNKS
HEADS = D // PLANES
EARLY = 896
LATE = (HALF - EARLY) // 2
MESH = pl.DeviceIdType.MESH
BF16 = jnp.bfloat16
F32 = jnp.float32


def attend_kernel(ids, usable, q_ref, *refs):
    kv, o_ref = refs[:WINDOW], refs[WINDOW]
    block = pl.program_id(0)
    heads = q_ref.shape[1] // HEAD_SIZE
    q = jnp.concatenate([q_ref[:, h * HEAD_SIZE : (h + 1) * HEAD_SIZE] for h in range(heads)], axis=0)
    keys = jnp.concatenate([kv[j][0, :, :HEAD_SIZE] for j in range(WINDOW)], axis=0)
    values = jnp.concatenate([kv[j][0, :, HEAD_SIZE:] for j in range(WINDOW)], axis=0)
    scores = lax.dot_general(q, keys, (((1,), (1,)), ((), ())), preferred_element_type=F32)
    scores = scores * HEAD_SIZE ** (-0.5)
    row = lax.broadcasted_iota(jnp.int32, (heads * BLOCK_TOKENS, BLOCK_TOKENS), 0) % BLOCK_TOKENS
    col = lax.broadcasted_iota(jnp.int32, (heads * BLOCK_TOKENS, BLOCK_TOKENS), 1)
    parts, masks = [], []
    for j in range(WINDOW):
        part = scores[:, j * BLOCK_TOKENS : (j + 1) * BLOCK_TOKENS]
        seen = jnp.full(part.shape, usable[block * WINDOW + j], jnp.int32) > 0
        if j == 0:
            seen = seen & (col <= row)
        parts.append(jnp.where(seen, part, -1e30))
        masks.append(seen)
    top = parts[0]
    for part in parts[1:]:
        top = jnp.maximum(top, part)
    top = jnp.max(top, axis=1, keepdims=True)
    parts = [jnp.where(seen, jnp.exp(part - top), 0.0) for part, seen in zip(parts, masks)]
    total = parts[0]
    for part in parts[1:]:
        total = total + part
    total = jnp.sum(total, axis=1, keepdims=True)
    probs = jnp.concatenate([(part / total).astype(BF16) for part in parts], axis=1)
    result = jnp.dot(probs, values, preferred_element_type=F32).astype(BF16)
    for h in range(heads):
        o_ref[:, h * HEAD_SIZE : (h + 1) * HEAD_SIZE] = result[h * BLOCK_TOKENS : (h + 1) * BLOCK_TOKENS]


def attend(queries, kv_blocks, ids, usable):
    blocks = queries.shape[0] // BLOCK_TOKENS
    width = queries.shape[1]

    def kv_spec(j):
        return pl.BlockSpec((1, BLOCK_TOKENS, 2 * HEAD_SIZE), lambda i, ids, usable: (ids[i * WINDOW + j], 0, 0))

    return pl.pallas_call(
        attend_kernel,
        grid_spec=pltpu.PrefetchScalarGridSpec(
            num_scalar_prefetch=2,
            grid=(blocks,),
            in_specs=[pl.BlockSpec((BLOCK_TOKENS, width), lambda i, ids, usable: (i, 0))]
            + [kv_spec(j) for j in range(WINDOW)],
            out_specs=pl.BlockSpec((BLOCK_TOKENS, width), lambda i, ids, usable: (i, 0)),
        ),
        out_shape=jax.ShapeDtypeStruct(queries.shape, BF16),
        compiler_params=pltpu.CompilerParams(vmem_limit_bytes=60 * 2**20),
        name="attend",
    )(ids, usable, queries, *([kv_blocks] * WINDOW))


def gather_kernel(own, w_own, kv, w_got, w_stage, s_s, s_r, b_s, b_r, o_s, x_s, x_r):
    ctx = lax.axis_index("ctx")
    z = lax.axis_index("exp")
    chip, c = lax.div(ctx, 2), lax.rem(ctx, 2)
    place = (lax.div(chip, GRID), lax.rem(chip, GRID))
    sibling = chip * 2 + 1 - c
    mate = lax.div(z, 2) * 2 + 1 - lax.rem(z, 2)
    same = c == lax.rem(z, 2)
    apart = c != lax.rem(z, 2)

    def chip_at(half, du, dv):
        u, v = place[half], place[1 - half]
        u, v = lax.rem(u + du + GRID, GRID), lax.rem(v + dv + GRID, GRID)
        return u * GRID + v if half == 0 else v * GRID + u

    def copy(src, dst, a_sem, b_sem, to_ctx, to_z):
        return pltpu.make_async_remote_copy(
            src_ref=src, dst_ref=dst, send_sem=a_sem, recv_sem=b_sem,
            device_id=(to_ctx, to_z), device_id_type=MESH,
        )

    barrier = pltpu.get_barrier_semaphore()

    def greet(cx, zz):
        pl.semaphore_signal(barrier, inc=1, device_id=(cx, zz), device_id_type=MESH)

    for half in range(2):
        for du in (1, -1):
            greet(chip_at(half, du, 0) * 2 + c, z)
    greet(sibling, z)
    greet(sibling, mate)
    greet(ctx, mate)
    pl.semaphore_wait(barrier, 7)

    first, second = pl.ds(0, EARLY // 2), pl.ds(EARLY // 2, EARLY // 2)

    def straight():
        return copy(w_own.at[first, :], w_got.at[first, :], x_s.at[0], x_r.at[0], sibling, mate)

    def to_stage():
        return copy(w_own.at[second, :], w_stage, x_s.at[1], x_r.at[1], sibling, z)

    def from_stage():
        return copy(w_stage, w_got.at[second, :], x_s.at[2], x_r.at[2], ctx, mate)

    @pl.when(apart)
    def _():
        to_stage().start()
        straight().start()

    started = []

    def launch(src, half, blocks, first, at, du, dv):
        to = chip_at(half, du, dv) * 2 + c
        dst = kv.at[at * 2 + c, pl.ds(first, blocks)]
        copy(src, dst, s_s.at[0], s_r.at[at, first], to, z).start()
        started.append(blocks)

    def held(at, first, blocks):
        return kv.at[at * 2 + c, pl.ds(first, blocks)]

    def arrive(at, first, blocks):
        ref = held(at, first, blocks)
        copy(ref, ref, s_s.at[0], s_r.at[at, first], ctx, z).wait_recv()

    def share(src, at, half):
        dst = kv.at[at * 2 + c, pl.ds(2 * half, 2)]
        copy(src, dst, b_s.at[0], b_r.at[0], sibling, z).start()

    for half in range(2):
        for du in (1, -1):
            launch(own.at[pl.ds(2 * half, 2)], half, 2, 2 * half, chip, du, 0)
    for half in range(2):
        for dv in (1, -1):
            launch(own.at[pl.ds(2 * half, 2)], half, 2, 2 * half, chip, 0, dv)
    for half in range(2):
        share(own.at[pl.ds(2 * half, 2)], chip, half)
    mine = pltpu.make_async_copy(own, kv.at[ctx], o_s.at[0])
    mine.start()

    def onward(half, du):
        at = chip_at(half, du, 0)
        for dv in (1, -1):
            launch(held(at, 2 * half, 2), half, 2, 2 * half, at, 0, dv)
        share(held(at, 2 * half, 2), at, half)

    for half in range(2):
        before, after = chip_at(half, -1, 0), chip_at(half, 1, 0)
        arrive(before, 2 * half, 2)
        launch(held(before, 2 * half, 1), half, 1, 2 * half, before, 1, 0)
        arrive(after, 2 * half, 2)
        launch(held(after, 2 * half + 1, 1), half, 1, 2 * half + 1, after, -1, 0)

    @pl.when(same)
    def _():
        to_stage().wait_recv()
        from_stage().start()

    for half in range(2):
        onward(half, -1)
        onward(half, 1)
    for half in range(2):
        far = chip_at(half, 2, 0)
        arrive(far, 2 * half, 1)
        arrive(far, 2 * half + 1, 1)
        onward(half, 2)
    for du in (0, -1, 1, 2):
        for half in range(2):
            before, after = chip_at(half, du, -1), chip_at(half, du, 1)
            arrive(before, 2 * half, 2)
            launch(held(before, 2 * half, 1), half, 1, 2 * half, before, 0, 1)
            arrive(after, 2 * half, 2)
            launch(held(after, 2 * half + 1, 1), half, 1, 2 * half + 1, after, 0, -1)
            share(held(before, 2 * half, 2), before, half)
            share(held(after, 2 * half, 2), after, half)
    for du in (0, -1, 1, 2):
        for half in range(2):
            far = chip_at(half, du, 2)
            arrive(far, 2 * half, 1)
            arrive(far, 2 * half + 1, 1)
            share(held(far, 2 * half, 2), far, half)

    def all_of(spans, s_sem, r_sem):
        return copy(kv.at[pl.ds(0, spans)], kv.at[pl.ds(0, spans)], s_sem.at[0], r_sem.at[0], sibling, z)

    all_of(CHIPS, b_s, b_r).wait_recv()
    all_of(CHIPS, b_s, b_r).wait_send()
    assert sum(started) % kv.shape[1] == 0
    all_of(sum(started) // kv.shape[1], s_s, b_r).wait_send()

    @pl.when(apart)
    def _():
        straight().wait()
        to_stage().wait_send()
        from_stage().wait_recv()

    @pl.when(same)
    def _():
        from_stage().wait_send()

    mine.wait()


def gather(own_kv, w_own):
    vmem = pl.BlockSpec(memory_space=pltpu.VMEM)
    hbm = pl.BlockSpec(memory_space=pl.ANY)
    dma = pltpu.SemaphoreType.DMA
    blocks = own_kv.shape[0]
    return pl.pallas_call(
        gather_kernel,
        out_shape=(
            jax.ShapeDtypeStruct((2 * CHIPS,) + own_kv.shape, BF16),
            jax.ShapeDtypeStruct((EARLY, 2 * FF), BF16),
            jax.ShapeDtypeStruct((EARLY // 2, 2 * FF), BF16),
        ),
        in_specs=[vmem, hbm],
        out_specs=(hbm, hbm, hbm),
        scratch_shapes=[
            dma((1,)), dma((CHIPS, blocks)),
            dma((1,)), dma((1,)),
            dma((1,)),
            dma((3,)), dma((3,)),
        ],
        compiler_params=pltpu.CompilerParams(collective_id=1, has_side_effects=True),
        cost_estimate=pl.CostEstimate(flops=0, bytes_accessed=100 * 10**6, transcendentals=0),
        name="gather",
    )(own_kv, w_own)


def expert_kernel(
    attn, resid, gain, route, w_own, w_got, w_out, out,
    routes, pos_in, pos_out, share_out, stage, heads_in, gath, toks, hot, sent, rows, win, wout, mine, theirs, hid_out, hid, back, comb, sib, parts,
    a_s, a_r, r_s, r_r, l_s, l_r, c_s, c_r, d_s, d_r, p_s, p_r, h_s, h_r, o_s, o_r, u_s, u_r, z_s, z_r, w_s, x_s, x_r, t_s, t_r,
):
    ctx = lax.axis_index("ctx")
    z = lax.axis_index("exp")
    chip, c = lax.div(ctx, 2), lax.rem(ctx, 2)
    x, y = lax.div(chip, GRID), lax.rem(chip, GRID)
    sibling = chip * 2 + 1 - c
    mate = lax.div(z, 2) * 2 + 1 - lax.rem(z, 2)
    same = c == lax.rem(z, 2)
    apart = c != lax.rem(z, 2)

    def send(src, dst, s_sem, r_sem, to_ctx, to_z):
        return pltpu.make_async_remote_copy(
            src_ref=src, dst_ref=dst, send_sem=s_sem, recv_sem=r_sem,
            device_id=(to_ctx, to_z), device_id_type=MESH,
        )

    def loop(count, body):
        lax.fori_loop(0, count, lambda i, carry: (body(i), carry)[1], 0)

    def mod8(v):
        return lax.rem(v + 2 * PLANES, PLANES)

    barrier = pltpu.get_barrier_semaphore()

    def greet(cx, zz):
        pl.semaphore_signal(barrier, inc=1, device_id=(cx, zz), device_id_type=MESH)

    def greet_chip(d):
        @pl.when(d != chip)
        def _():
            greet(d * 2 + c, z)

    loop(CHIPS, greet_chip)
    loop(PLANES - 1, lambda r: greet(ctx, mod8(z + r + 1)))
    greet(sibling, z)
    greet(sibling, mate)

    early, late = pl.ds(0, EARLY), pl.ds(EARLY, HALF - EARLY)
    straight, around = pl.ds(EARLY, LATE), pl.ds(EARLY + LATE, LATE)

    def win_copy(ref):
        return pltpu.make_async_copy(ref.at[early, :], win.at[early, :], w_s.at[0])

    def win_late():
        return pltpu.make_async_copy(w_own.at[late, :], win.at[late, :], w_s.at[1])

    def wout_copy(k):
        return pltpu.make_async_copy(w_out.at[:, pl.ds(k * CHUNK, CHUNK)], wout.at[k], w_s.at[2])

    def swap_late():
        return send(w_own.at[straight, :], win.at[straight, :], x_s.at[0], x_r.at[0], sibling, mate)

    def to_stage():
        return send(w_own.at[around, :], stage, x_s.at[1], x_r.at[1], sibling, z)

    def from_stage():
        return send(stage, win.at[around, :], x_s.at[2], x_r.at[2], ctx, mate)

    @pl.when(same)
    def _():
        win_copy(w_own).start()
        win_late().start()

    @pl.when(apart)
    def _():
        win_copy(w_got).start()

    for k in range(CHUNKS):
        wout_copy(k).start()

    def above(b):
        at = pl.ds(pl.multiple_of(b * 128, 128), 128)
        row = lax.broadcasted_iota(jnp.int32, (128, COLUMN), 0) + b * 128
        col = lax.broadcasted_iota(jnp.int32, (128, COLUMN), 1)
        mine[at, 0:COLUMN] = jnp.where(row < col, 1.0, 0.0).astype(BF16)

    loop(COLUMN // 128, above)
    pl.semaphore_wait(barrier, (CHIPS - 1) + (PLANES - 1) + 2)

    def a_send(r):
        to = mod8(z + r + 1)
        return send(attn.at[pl.ds(pl.multiple_of(to * TOK, TOK), TOK), :], heads_in.at[z], a_s.at[0], a_r.at[0], ctx, to)

    def tokens_of(core):
        return pl.ds(pl.multiple_of(core * SPAN, SPAN), SPAN)

    def place(core, slot):
        return pl.ds(pl.multiple_of(core * SPAN + slot * TOK, TOK), TOK)

    def t_send(r):
        to = mod8(z + r + 1)
        return send(route, routes.at[place(c, z), :], t_s.at[0], t_r.at[0], ctx, to)

    def t_across(core):
        at = tokens_of(core)
        return send(routes.at[at, :], routes.at[at, :], t_s.at[1], t_r.at[1], sibling, z)

    loop(PLANES - 1, lambda r: a_send(r).start())
    heads_in[z] = attn[pl.ds(pl.multiple_of(z * TOK, TOK), TOK), :]

    def a_all():
        ref = heads_in.at[pl.ds(0, PLANES - 1)]
        return send(ref, ref, a_s.at[0], a_r.at[0], ctx, z)

    a_all().wait_recv()

    squares = jnp.zeros((TOK, 1), F32)
    for b in range(PLANES):
        summed = resid[:, b * HEADS : (b + 1) * HEADS].astype(F32) + heads_in[b].astype(F32)
        squares = squares + jnp.sum(summed * summed, axis=1, keepdims=True)
    scale = lax.rsqrt(squares / D + 1e-06)

    def summed_at(b):
        at = slice(b * CHUNK, (b + 1) * CHUNK)
        plane, first = b * CHUNK // HEADS, b * CHUNK % HEADS
        return resid[:, at].astype(F32) + heads_in[plane, :, first : first + CHUNK].astype(F32)

    for b in range(2 * CHUNKS):
        normed = summed_at(b) * scale * gain[:, b * CHUNK : (b + 1) * CHUNK]
        gath[b % CHUNKS, z, b // CHUNKS] = normed.astype(BF16)

    def piece(k, r, slot, half):
        return gath.at[k, slot] if r < 4 else gath.at[k, slot, half]

    def right(k, r):
        ref = piece(k, r, mod8(z - r + 1), 0)
        return send(ref, ref, r_s.at[0], r_r.at[k, r - 1], ctx, mod8(z + 1))

    def left(k, r):
        ref = piece(k, r, mod8(z + r - 1), 1)
        return send(ref, ref, l_s.at[0], l_r.at[k, r - 1], ctx, mod8(z - 1))

    def right_in(k, r):
        ref = piece(k, r, mod8(z - r), 0)
        return send(ref, ref, r_s.at[0], r_r.at[k, r - 1], ctx, mod8(z + 1))

    def left_in(k, r):
        ref = piece(k, r, mod8(z + r), 1)
        return send(ref, ref, l_s.at[0], l_r.at[k, r - 1], ctx, mod8(z - 1))

    def across(k, slot):
        return send(
            gath.at[k, slot, 1 - c], toks.at[k, place(c, slot), :], c_s.at[0], c_r.at[k], sibling, z
        )

    def across_in(k):
        ref = toks.at[k, pl.ds(0, SPAN), :]
        return send(ref, ref, c_s.at[0], c_r.at[k], sibling, z)

    def arrived(k, slot):
        across(k, slot).start()
        toks[k, place(c, slot), :] = gath[k, slot, c]

    own = pl.ds(pl.multiple_of(chip * SLOTS, SLOTS), SLOTS)

    def d_send(k, d):
        at = pl.ds(pl.multiple_of(d * SLOTS, SLOTS), SLOTS)
        return send(sent.at[k, at, :], rows.at[own, pl.ds(k * CHUNK, CHUNK)], d_s.at[0], d_r.at[x], d * 2 + c, z)

    def dispatch(k):
        across_in(k).wait_recv()

        def step(g):
            xd = lax.rem(x + g, GRID)
            slot = lax.broadcasted_iota(jnp.int32, (SLOTS, COLUMN), 0)
            for i in range(GRID):
                hot[i * SLOTS : (i + 1) * SLOTS, :] = jnp.where(slot.astype(F32) == pos_in[xd * GRID + i], 1.0, 0.0).astype(BF16)
            at = pl.ds(pl.multiple_of(xd * GROUP, GROUP), GROUP)
            sent[k, at, :] = jnp.dot(hot[...], toks[k], preferred_element_type=F32).astype(BF16)
            for j in range(1, GRID):
                d_send(k, xd * GRID + lax.rem(y + j, GRID)).start()

            @pl.when(g > 0)
            def _():
                d_send(k, xd * GRID + y).start()

        loop(GRID, step)
        rows[own, k * CHUNK : (k + 1) * CHUNK] = sent[k, own, :]

    def lag(k):
        return k

    def t_all():
        ref = routes.at[pl.ds(0, (PLANES - 1) * TOK), :]
        return send(ref, ref, t_s.at[0], t_r.at[0], ctx, z)

    def ranks():
        table = jnp.transpose(routes[...])
        chips = lax.broadcasted_iota(jnp.int32, (CHIPS, COLUMN), 0) * PLANES + lax.div(z, 2)
        names_in = (chips + lax.rem(z, 2) * (PLANES // 2)).astype(F32)
        names_out = (chips + c * (PLANES // 2)).astype(F32)
        in_in, in_out = jnp.zeros((CHIPS, COLUMN), F32), jnp.zeros((CHIPS, COLUMN), F32)
        share = jnp.zeros((CHIPS, COLUMN), F32)
        for k in range(TOPK):
            named = table[k : k + 1]
            in_in = in_in + jnp.where(names_in == named, 1.0, 0.0)
            in_out = in_out + jnp.where(names_out == named, 1.0, 0.0)
            share = share + jnp.where(names_out == named, table[TOPK + k : TOPK + k + 1], 0.0)
        member = jnp.concatenate([in_in, in_out], axis=0)
        rank = jnp.dot(member.astype(BF16), mine[0:COLUMN, 0:COLUMN], preferred_element_type=F32)
        rank = jnp.where(member > 0.0, rank, -1.0)
        for d in range(CHIPS):
            pos_in[d] = rank[d : d + 1]
        blank = jnp.zeros((HEAD_SIZE - CHIPS, COLUMN), F32)
        pos_out[...] = jnp.transpose(jnp.concatenate([rank[CHIPS:], blank], axis=0)).astype(BF16)
        share_out[...] = jnp.transpose(jnp.concatenate([share, blank], axis=0)).astype(BF16)

    for tick in range(1, lag(CHUNKS - 1) + 6):
        for k in range(CHUNKS):
            r = tick - lag(k)
            if 2 <= r <= 5:
                right_in(k, r - 1).wait_recv()
                left_in(k, r - 1).wait_recv()
            if 1 <= r <= 4:
                right(k, r).start()
                left(k, r).start()
            if r == 1:
                arrived(k, z)
            if 2 <= r <= 4:
                arrived(k, mod8(z - r + 1))
                arrived(k, mod8(z + r - 1))
            if r == 5:
                arrived(k, mod8(z + 4))
        if tick == 1:
            loop(PLANES - 1, lambda r: t_send(r).start())
            routes[place(c, z), :] = route[...]

            @pl.when(apart)
            def _():
                to_stage().start()

        if tick == 2:
            t_all().wait_recv()
            t_across(c).start()
        if tick == 3:
            t_across(1 - c).wait_recv()
            ranks()
        for k in range(CHUNKS):
            if tick - lag(k) == 5:
                dispatch(k)
        if tick == CHUNKS + 3:

            @pl.when(apart)
            def _():
                swap_late().start()

            @pl.when(same)
            def _():
                to_stage().wait_recv()
                from_stage().start()

    lane = lax.broadcasted_iota(jnp.int32, (HEAD_SIZE, ROWS), 1)
    owner = lax.broadcasted_iota(jnp.int32, (HEAD_SIZE, ROWS), 0) * SLOTS
    spread = jnp.where((lane >= owner) & (lane < owner + SLOTS), 1.0, 0.0).astype(BF16)

    def build(b):
        at = pl.ds(pl.multiple_of(b * 128, 128), 128)
        slot = jnp.dot(pos_out[at, :], spread, preferred_element_type=F32)
        share = jnp.dot(share_out[at, :], spread, preferred_element_type=F32)
        want = lax.rem(lax.broadcasted_iota(jnp.int32, (128, ROWS), 1), SLOTS).astype(F32)
        comb[at, :] = jnp.where(slot == want, share, 0.0).astype(BF16)

    loop(COLUMN // 128, build)

    win_copy(w_own).wait()
    pltpu.make_async_copy(wout, wout, w_s.at[2]).wait()

    def span_of(g):
        xs = lax.rem(x - g + GRID, GRID)
        return xs, pl.ds(pl.multiple_of(xs * GROUP, GROUP), GROUP)

    def p_send(g):
        _, at = span_of(g)
        return send(mine.at[at, :], theirs.at[at, :], p_s.at[0], p_r.at[g], sibling, z)

    def first(g):
        xs, at = span_of(g)

        def from_row(count):
            ref = rows.at[pl.ds(0, count), :]
            send(ref, ref, d_s.at[0], d_r.at[xs], ctx, z).wait_recv()

        @pl.when(g == 0)
        def _():
            from_row(GROUP - SLOTS)

        @pl.when(g > 0)
        def _():
            from_row(GROUP)

        @pl.when((g == 0) & same)
        def _():
            win_late().wait()

        @pl.when((g == 0) & apart)
        def _():
            swap_late().wait_recv()
            from_stage().wait_recv()

        mine[at, :] = jnp.dot(rows[at, :], win[...], preferred_element_type=F32).astype(BF16)
        p_send(g).start()

    def h_send(g):
        at = pl.ds(pl.multiple_of(span_of(g)[0] * GROUP, GROUP), GROUP // 2)
        return send(hid_out.at[at, :], hid.at[at, :], h_s.at[0], h_r.at[g], sibling, mate)

    def h_same(g):
        at = pl.ds(pl.multiple_of(span_of(g)[0] * GROUP + GROUP // 2, GROUP // 2), GROUP // 2)
        return send(hid.at[at, :], hid.at[at, :], h_s.at[0], h_r.at[g], ctx, mate)

    def hidden(g):
        p_send(g).wait_recv()
        xs, _ = span_of(g)

        def part(i):
            at = pl.ds(pl.multiple_of(xs * GROUP + i * 32, 32), 32)
            pre = mine[at, :].astype(F32) + theirs[at, :].astype(F32)
            gate, up = pre[:, :FF], pre[:, FF:]
            value = (gate / (1.0 + jnp.exp(-gate)) * up).astype(BF16)

            @pl.when(same)
            def _():
                hid[at, :] = value

            @pl.when(apart)
            def _():
                hid_out[at, :] = value

        loop(GROUP // 32, part)

        @pl.when(apart)
        def _():
            h_send(g).start()

        @pl.when(same)
        def _():
            h_same(g).start()

    def first_and_hidden(g):
        @pl.when(g < GRID)
        def _():
            first(g)

        @pl.when(g > 0)
        def _():
            hidden(g - 1)

    loop(GRID + 1, first_and_hidden)

    def d_all(r_sem):
        ref = sent.at[:, pl.ds(0, ROWS - SLOTS), :]
        return send(ref, ref, d_s.at[0], r_sem, ctx, z)

    d_all(d_r.at[0]).wait_send()

    def o_send(n, d):
        at = pl.ds(pl.multiple_of(d * SLOTS, SLOTS), SLOTS)
        return send(sent.at[n, at, :], back.at[n, own, :], o_s.at[0], o_r.at[n], d * 2 + c, z)

    def second(n, g):
        xs, at = span_of(g)

        @pl.when((n == 0) & apart)
        def _():
            send(hid.at[at, :], hid.at[at, :], h_s.at[0], h_r.at[g], sibling, mate).wait_recv()

        sent[n, at, :] = jnp.dot(hid[at, :], wout[n], preferred_element_type=F32).astype(BF16)
        for j in range(1, GRID):
            o_send(n, xs * GRID + lax.rem(y + j, GRID)).start()

        @pl.when(g > 0)
        def _():
            o_send(n, xs * GRID + y).start()

        @pl.when(g == 0)
        def _():
            back[n, own, :] = sent[n, own, :]

    units = CHUNKS * 7 // 2 // 4
    for s_sem, r_sem in ((r_s, r_r), (l_s, l_r)):
        ref = gath.at[pl.ds(0, units), pl.ds(0, 4)]
        send(ref, ref, s_sem.at[0], r_sem.at[0, 0], ctx, z).wait_send()
    ref = gath.at[pl.ds(0, CHUNKS // 2)]
    send(ref, ref, c_s.at[0], c_r.at[0], ctx, z).wait_send()

    def u_send(n):
        return send(toks.at[n, pl.ds(0, SPAN), :], sib.at[n], u_s.at[0], u_r.at[n], sibling, z)

    def z_send(n, to):
        return send(gath.at[n, to, 0], parts.at[n, z], z_s.at[0], z_r.at[n], ctx, to)

    def combine(step):
        @pl.when(step < CHUNKS)
        def _():
            loop(GRID, lambda g: second(step, g))

        @pl.when(step > 1)
        def _():
            n = step - 2

            ref = back.at[n, pl.ds(0, ROWS - SLOTS), :]
            send(ref, ref, o_s.at[0], o_r.at[n], ctx, z).wait_recv()
            toks[n, pl.ds(0, SPAN), :] = jnp.dot(
                comb[tokens_of(1 - c), :], back[n], preferred_element_type=F32
            ).astype(BF16)
            u_send(n).start()
            total = jnp.dot(comb[tokens_of(c), :], back[n], preferred_element_type=F32)
            u_send(n).wait_recv()
            total = (total + sib[n].astype(F32)).astype(BF16)
            for s in range(PLANES):
                gath[n, s, 0] = total[s * TOK : (s + 1) * TOK]
            loop(PLANES - 1, lambda r: z_send(n, mod8(z + r + 1)).start())
            parts[n, z] = gath[n, z, 0]

    loop(CHUNKS + 2, combine)

    for n in range(CHUNKS):
        ref = parts.at[n, pl.ds(0, PLANES - 1)]
        send(ref, ref, z_s.at[0], z_r.at[n], ctx, z).wait_recv()
        for half in range(2):
            b = half * CHUNKS + n
            total = parts[n, half].astype(F32)
            for q in range(1, PLANES // 2):
                total = total + parts[n, 2 * q + half].astype(F32)
            out[:, b * CHUNK : (b + 1) * CHUNK] = (summed_at(b) + total).astype(BF16)

    a_all().wait_send()
    send(mine, mine, p_s.at[0], p_r.at[0], ctx, z).wait_send()
    ref = hid.at[pl.ds(0, ROWS // 2), :]
    send(ref, ref, h_s.at[0], h_r.at[0], ctx, z).wait_send()
    ref = sent.at[:, pl.ds(0, ROWS - SLOTS), :]
    send(ref, ref, o_s.at[0], o_r.at[0], ctx, z).wait_send()
    ref = toks.at[:, pl.ds(0, SPAN), :]
    send(ref, ref, u_s.at[0], u_r.at[0], ctx, z).wait_send()
    ref = parts.at[:, pl.ds(0, PLANES - 1)]
    send(ref, ref, z_s.at[0], z_r.at[0], ctx, z).wait_send()

    @pl.when(apart)
    def _():
        swap_late().wait_send()
        to_stage().wait_send()

    @pl.when(same)
    def _():
        from_stage().wait_send()

    t_all().wait_send()
    t_across(c).wait_send()


def run_experts(attn, resid, gain, route, w_own, w_got, w_out):
    vmem = pl.BlockSpec(memory_space=pltpu.VMEM)
    hbm = pl.BlockSpec(memory_space=pl.ANY)
    dma = pltpu.SemaphoreType.DMA
    return pl.pallas_call(
        expert_kernel,
        out_shape=jax.ShapeDtypeStruct((TOK, D), BF16),
        in_specs=[vmem] * 4 + [hbm] * 3,
        out_specs=vmem,
        scratch_shapes=[
            pltpu.VMEM((COLUMN, HEAD_SIZE), F32),
            pltpu.VMEM((CHIPS, 1, COLUMN), F32),
            pltpu.VMEM((COLUMN, HEAD_SIZE), BF16),
            pltpu.VMEM((COLUMN, HEAD_SIZE), BF16),
            pltpu.VMEM((LATE, 2 * FF), BF16),
            pltpu.VMEM((PLANES, TOK, HEADS), BF16),
            pltpu.VMEM((CHUNKS, PLANES, 2, TOK, CHUNK), BF16),
            pltpu.VMEM((CHUNKS, COLUMN, CHUNK), BF16),
            pltpu.VMEM((GROUP, COLUMN), BF16),
            pltpu.VMEM((CHUNKS, ROWS, CHUNK), BF16),
            pltpu.VMEM((ROWS, HALF), BF16),
            pltpu.VMEM((HALF, 2 * FF), BF16),
            pltpu.VMEM((CHUNKS, FF, CHUNK), BF16),
            pltpu.VMEM((ROWS, 2 * FF), BF16),
            pltpu.VMEM((ROWS, 2 * FF), BF16),
            pltpu.VMEM((ROWS, FF), BF16),
            pltpu.VMEM((ROWS, FF), BF16),
            pltpu.VMEM((CHUNKS, ROWS, CHUNK), BF16),
            pltpu.VMEM((COLUMN, ROWS), BF16),
            pltpu.VMEM((CHUNKS, SPAN, CHUNK), BF16),
            pltpu.VMEM((CHUNKS, PLANES, TOK, CHUNK), BF16),
            dma((1,)), dma((1,)),
            dma((1,)), dma((CHUNKS, 4)),
            dma((1,)), dma((CHUNKS, 4)),
            dma((1,)), dma((CHUNKS,)),
            dma((1,)), dma((GRID,)),
            dma((1,)), dma((GRID,)),
            dma((1,)), dma((GRID,)),
            dma((1,)), dma((CHUNKS,)),
            dma((1,)), dma((CHUNKS,)),
            dma((1,)), dma((CHUNKS,)),
            dma((3,)),
            dma((3,)), dma((3,)),
            dma((2,)), dma((2,)),
        ],
        compiler_params=pltpu.CompilerParams(
            collective_id=0, has_side_effects=True, vmem_limit_bytes=62 * 2**20
        ),
        cost_estimate=pl.CostEstimate(flops=25 * 10**9, bytes_accessed=12 * 10**6, transcendentals=10**6),
        name="experts",
    )(attn, resid, gain, route, w_own, w_got, w_out)


def local(
    queries, key_value_stack, vertical_cols, slash_offsets, resid,
    norm_gain, expert_ids, gate_weights, w_in, w_out,
):
    ctx = lax.axis_index("ctx")
    z = lax.axis_index("exp")
    blocks = queries.shape[0] // BLOCK_TOKENS
    heads_dev = queries.shape[1] // HEAD_SIZE

    kv_head = z * heads_dev // (QUERY_HEADS // KEY_VALUE_HEADS)
    own_kv = lax.dynamic_slice_in_dim(key_value_stack, kv_head * HEAD_SIZE, HEAD_SIZE, 2)
    own_kv = own_kv.reshape(blocks, BLOCK_TOKENS, 2 * HEAD_SIZE)

    w_own = w_in[0]

    shares = gate_weights / jnp.sum(gate_weights, axis=1, keepdims=True)
    routing = jnp.concatenate([expert_ids.astype(F32), shares], axis=1)
    routing = jnp.pad(routing, ((0, 0), (0, HEAD_SIZE - 2 * TOPK)))
    kv, w_got, _ = gather(own_kv, w_own)
    kv_blocks = kv.reshape(-1, BLOCK_TOKENS, 2 * HEAD_SIZE)

    first = ctx * blocks
    cols = lax.dynamic_slice_in_dim(vertical_cols, first, blocks, 0)
    offsets = lax.dynamic_slice_in_dim(slash_offsets, first, blocks, 0)
    slash = (first + jnp.arange(blocks, dtype=jnp.int32))[:, None] - offsets
    in_slash = jnp.any(cols[:, :, None] == slash[:, None, :], axis=2)
    earlier = jnp.arange(NV)[None, :] < jnp.arange(NV)[:, None]
    repeated = jnp.any((cols[:, :, None] == cols[:, None, :]) & earlier[None], axis=2)
    usable = jnp.concatenate([slash >= 0, (cols >= 0) & ~in_slash & ~repeated], axis=1)
    chosen = jnp.maximum(jnp.concatenate([slash, cols], axis=1), 0)
    attn = attend(queries, kv_blocks, chosen.reshape(-1), usable.astype(jnp.int32).reshape(-1))

    return run_experts(attn, resid, norm_gain[None, :], routing, w_own, w_got, w_out[0])


def solution(mesh):
    in_specs = (
        P("ctx", "exp"),
        P("ctx", None, None),
        P(),
        P(),
        P(("ctx", "exp"), None),
        P(),
        P(("ctx", "exp"), None),
        P(("ctx", "exp"), None),
        P(("ctx", "exp"), None, None),
        P(("ctx", "exp"), None, None),
    )
    out_specs = P(("ctx", "exp"), None)
    return jax.shard_map(local, mesh=mesh, in_specs=in_specs, out_specs=out_specs, check_vma=False)
```

```python
import jax
import jax.numpy as jnp
from jax import lax
from jax.experimental import pallas as pl
from jax.experimental.pallas import tpu as pltpu
from jax.sharding import PartitionSpec as P

D = 4096
QUERY_HEADS = 32
KEY_VALUE_HEADS = 4
HEAD_SIZE = 128
FF = 768
TOPK = 8
BLOCK_TOKENS = 128
NV = 4
NS = 2
WINDOW = NS + NV

GRID = 4
CHIPS = GRID * GRID
PLANES = 8
TOK = 64
SPAN = PLANES * TOK
COLUMN = 2 * SPAN
CAP = 5
SLOTS = CAP * 2 * PLANES
GROUP = GRID * SLOTS
ROWS = CHIPS * SLOTS
HALF = D // 2
CHUNKS = 8
CHUNK = HALF // CHUNKS
HEADS = D // PLANES
PIECES = 16
PIECE = HALF // 2 // PIECES
EARLY = 5
RING = (5, 6, 7, 8, 9, 10, 11)
LAPS = tuple((k, 1) for k in range(CHUNKS))
VMEM_BYTES = 63 * 2**20
MESH = pl.DeviceIdType.MESH
BF16 = jnp.bfloat16
F32 = jnp.float32


def attend(q, kv, seen_blocks):
    heads = q.shape[1] // HEAD_SIZE
    q = jnp.concatenate([q[:, h * HEAD_SIZE : (h + 1) * HEAD_SIZE] for h in range(heads)], axis=0)
    keys = jnp.concatenate([block[:, :HEAD_SIZE] for block in kv], axis=0)
    values = jnp.concatenate([block[:, HEAD_SIZE:] for block in kv], axis=0)
    scores = lax.dot_general(q, keys, (((1,), (1,)), ((), ())), preferred_element_type=F32)
    scores = scores * HEAD_SIZE ** (-0.5)
    row = lax.broadcasted_iota(jnp.int32, (heads * BLOCK_TOKENS, BLOCK_TOKENS), 0) % BLOCK_TOKENS
    col = lax.broadcasted_iota(jnp.int32, (heads * BLOCK_TOKENS, BLOCK_TOKENS), 1)
    parts, masks = [], []
    for j in range(WINDOW):
        part = scores[:, j * BLOCK_TOKENS : (j + 1) * BLOCK_TOKENS]
        seen = jnp.full(part.shape, seen_blocks[j], jnp.int32) > 0
        if j == 0:
            seen = seen & (col <= row)
        parts.append(jnp.where(seen, part, -1e30))
        masks.append(seen)
    top = parts[0]
    for part in parts[1:]:
        top = jnp.maximum(top, part)
    top = jnp.max(top, axis=1, keepdims=True)
    parts = [jnp.where(seen, jnp.exp(part - top), 0.0) for part, seen in zip(parts, masks)]
    total = parts[0]
    for part in parts[1:]:
        total = total + part
    total = jnp.sum(total, axis=1, keepdims=True)
    probs = jnp.concatenate([(part / total).astype(BF16) for part in parts], axis=1)
    result = jnp.dot(probs, values, preferred_element_type=F32).astype(BF16)
    return jnp.concatenate([result[h * BLOCK_TOKENS : (h + 1) * BLOCK_TOKENS] for h in range(heads)], axis=1)


def layer_kernel(
    cols, offsets, own, queries, ids, gates, resid, gain, w_own, w_out, out, w_stage,
    kv, route, routes, pos_in, pos_out, share_out, heads_in, gath, toks, hot, rows, win, wout,
    mine, theirs, hid_out, hid, back, comb, sib, parts,
    s_s, s_r, b_s, b_r, o_c, a_s, a_r, t_s, t_r,
    r_s, r_r, l_s, l_r, c_s, c_r, d_s, d_r, p_s, p_r, h_s, h_r, o_s, o_r, u_s, u_r, z_s, z_r, w_s, x_s, x_r,
):
    ctx = lax.axis_index("ctx")
    z = lax.axis_index("exp")
    chip, c = lax.div(ctx, 2), lax.rem(ctx, 2)
    x, y = lax.div(chip, GRID), lax.rem(chip, GRID)
    sibling = chip * 2 + 1 - c
    mate = lax.div(z, 2) * 2 + 1 - lax.rem(z, 2)
    same = c == lax.rem(z, 2)
    apart = c != lax.rem(z, 2)

    def send(src, dst, s_sem, r_sem, to_ctx, to_z):
        return pltpu.make_async_remote_copy(
            src_ref=src, dst_ref=dst, send_sem=s_sem, recv_sem=r_sem,
            device_id=(to_ctx, to_z), device_id_type=MESH,
        )

    def loop(count, body):
        lax.fori_loop(0, count, lambda i, carry: (body(i), carry)[1], 0)

    def mod8(v):
        return lax.rem(v + 2 * PLANES, PLANES)

    barrier = pltpu.get_barrier_semaphore()

    def greet(cx, zz):
        pl.semaphore_signal(barrier, inc=1, device_id=(cx, zz), device_id_type=MESH)

    def greet_chip(d):
        @pl.when(d != chip)
        def _():
            greet(d * 2 + c, z)

    loop(CHIPS, greet_chip)
    loop(PLANES - 1, lambda r: greet(ctx, mod8(z + r + 1)))
    greet(sibling, z)
    greet(sibling, mate)

    def wout_copy(k):
        return pltpu.make_async_copy(w_out.at[:, pl.ds(k * CHUNK, CHUNK)], wout.at[k], w_s.at[1])

    def piece_rows(first, p):
        return pl.ds(pl.multiple_of(first + p * PIECE, PIECE), PIECE)

    def straight(p):
        at = piece_rows(0, p)
        return send(w_own.at[at, :], win.at[at, :], x_s.at[0], x_r.at[0], sibling, mate)

    def to_stage():
        return send(w_own.at[pl.ds(HALF // 2, HALF // 2), :], w_stage, x_s.at[1], x_r.at[1], sibling, z)

    def from_stage(p):
        src, dst = piece_rows(0, p), piece_rows(HALF // 2, p)
        return send(w_stage.at[src, :], win.at[dst, :], x_s.at[2], x_r.at[2], ctx, mate)

    def next_piece(p):
        @pl.when(apart)
        def _():
            straight(p).start()

        @pl.when(same)
        def _():
            from_stage(p).start()

    @pl.when(same)
    def _():
        pltpu.make_async_copy(w_own, win, w_s.at[0]).start()

    for k in range(CHUNKS):
        wout_copy(k).start()

    def above(b):
        at = pl.ds(pl.multiple_of(b * 128, 128), 128)
        row = lax.broadcasted_iota(jnp.int32, (128, COLUMN), 0) + b * 128
        col = lax.broadcasted_iota(jnp.int32, (128, COLUMN), 1)
        mine[at, 0:COLUMN] = jnp.where(row < col, 1.0, 0.0).astype(BF16)

    loop(COLUMN // 128, above)

    def tokens_of(core):
        return pl.ds(pl.multiple_of(core * SPAN, SPAN), SPAN)

    def place(core, slot):
        return pl.ds(pl.multiple_of(core * SPAN + slot * TOK, TOK), TOK)

    shares = gates[...] / jnp.sum(gates[...], axis=0, keepdims=True)
    blank = jnp.zeros((HEAD_SIZE - 2 * TOPK, TOK), F32)
    both = jnp.concatenate([ids[...].astype(F32), shares, blank], axis=0)
    both = jnp.concatenate([both, jnp.zeros((HEAD_SIZE, HEAD_SIZE - TOK), F32)], axis=1)
    route[...] = jnp.transpose(both)[:TOK]
    routes[place(c, z), :] = route[...]

    def t_send(to):
        return send(route, routes.at[place(c, z), :], t_s.at[0], t_r.at[0], ctx, to)

    def t_all():
        ref = routes.at[pl.ds(0, (PLANES - 1) * TOK), :]
        return send(ref, ref, t_s.at[0], t_r.at[0], ctx, z)

    def t_across(core):
        at = tokens_of(core)
        return send(routes.at[at, :], routes.at[at, :], t_s.at[1], t_r.at[1], sibling, z)

    spot = (x, y)

    def chip_at(half, du, dv):
        u, v = spot[half], spot[1 - half]
        u, v = lax.rem(u + du + GRID, GRID), lax.rem(v + dv + GRID, GRID)
        return u * GRID + v if half == 0 else v * GRID + u

    pl.semaphore_wait(barrier, (CHIPS - 1) + (PLANES - 1) + 2)

    per = SPAN // BLOCK_TOKENS
    started = []

    def blocks_at(first, count):
        return kv.at[pl.ds(first, count)]

    def own_at(first, count):
        return own.at[pl.ds(first, count)]

    def launch(src, half, blocks, first, at, du, dv):
        to = chip_at(half, du, dv) * 2 + c
        dst = blocks_at((at * 2 + c) * per + first, blocks)
        send(src, dst, s_s.at[0], s_r.at[at, first], to, z).start()
        started.append(blocks)

    def held(at, first, blocks):
        return blocks_at((at * 2 + c) * per + first, blocks)

    def arrive(at, first, blocks):
        ref = held(at, first, blocks)
        send(ref, ref, s_s.at[0], s_r.at[at, first], ctx, z).wait_recv()

    def share(src, at, half):
        dst = blocks_at((at * 2 + c) * per + 2 * half, 2)
        send(src, dst, b_s.at[0], b_r.at[0], sibling, z).start()

    for half in range(2):
        for du in (1, -1):
            launch(own_at(2 * half, 2), half, 2, 2 * half, chip, du, 0)
    for half in range(2):
        for dv in (1, -1):
            launch(own_at(2 * half, 2), half, 2, 2 * half, chip, 0, dv)
    for half in range(2):
        share(own_at(2 * half, 2), chip, half)
    own_copy = pltpu.make_async_copy(own, blocks_at(ctx * per, per), o_c.at[0])
    own_copy.start()
    loop(PLANES - 1, lambda r: t_send(mod8(z + r + 1)).start())

    @pl.when(apart)
    def _():
        to_stage().start()
        loop(EARLY, lambda p: straight(p).start())

    def onward(half, du):
        at = chip_at(half, du, 0)
        for dv in (1, -1):
            launch(held(at, 2 * half, 2), half, 2, 2 * half, at, 0, dv)
        share(held(at, 2 * half, 2), at, half)

    for half in range(2):
        before, after = chip_at(half, -1, 0), chip_at(half, 1, 0)
        arrive(before, 2 * half, 2)
        launch(held(before, 2 * half, 1), half, 1, 2 * half, before, 1, 0)
        arrive(after, 2 * half, 2)
        launch(held(after, 2 * half + 1, 1), half, 1, 2 * half + 1, after, -1, 0)

    @pl.when(same)
    def _():
        to_stage().wait_recv()
        loop(EARLY, lambda p: from_stage(p).start())

    for half in range(2):
        onward(half, -1)
        onward(half, 1)
    t_all().wait_recv()
    t_across(c).start()
    for half in range(2):
        far = chip_at(half, 2, 0)
        arrive(far, 2 * half, 1)
        arrive(far, 2 * half + 1, 1)
        onward(half, 2)
    for du in (0, -1, 1, 2):
        for half in range(2):
            before, after = chip_at(half, du, -1), chip_at(half, du, 1)
            arrive(before, 2 * half, 2)
            launch(held(before, 2 * half, 1), half, 1, 2 * half, before, 0, 1)
            arrive(after, 2 * half, 2)
            launch(held(after, 2 * half + 1, 1), half, 1, 2 * half + 1, after, 0, -1)
            share(held(before, 2 * half, 2), before, half)
            share(held(after, 2 * half, 2), after, half)
    for du in (0, -1, 1, 2):
        for half in range(2):
            far = chip_at(half, du, 2)
            arrive(far, 2 * half, 1)
            arrive(far, 2 * half + 1, 1)
            share(held(far, 2 * half, 2), far, half)

    def all_of(blocks, s_sem, r_sem):
        ref = blocks_at(0, blocks)
        return send(ref, ref, s_sem.at[0], r_sem.at[0], sibling, z)

    all_of(CHIPS * per, b_s, b_r).wait_recv()
    own_copy.wait()

    def a_send(to):
        at = pl.ds(pl.multiple_of(to * TOK, TOK), TOK)
        return send(comb.at[at, pl.ds(0, HEADS)], heads_in.at[z], a_s.at[0], a_r.at[0], ctx, to)

    def block(turn, carry):
        i = lax.rem(turn + lax.div(z, 2) + 1, SPAN // BLOCK_TOKENS)
        at = pl.ds(pl.multiple_of(i * BLOCK_TOKENS, BLOCK_TOKENS), BLOCK_TOKENS)
        number = ctx * per + i
        slash = [number - offsets[j, number] for j in range(NS)]
        column = [cols[j, number] for j in range(NV)]
        kept = [v >= 0 for v in slash]
        for j in range(NV):
            keep = column[j] >= 0
            for other in slash + column[:j]:
                keep = jnp.logical_and(keep, column[j] != other)
            kept.append(keep)
        chosen = [kv[jnp.maximum(v, 0)] for v in slash + column]
        kept = [jnp.where(v, 1, 0) for v in kept]
        comb[at, 0:HEADS] = attend(queries[at, :], chosen, kept)
        for part in range(BLOCK_TOKENS // TOK):
            to = i * (BLOCK_TOKENS // TOK) + part

            @pl.when(to != z)
            def _():
                a_send(to).start()

        return carry

    lax.fori_loop(0, SPAN // BLOCK_TOKENS, block, 0)
    heads_in[z] = comb[pl.ds(pl.multiple_of(z * TOK, TOK), TOK), 0:HEADS]

    t_across(1 - c).wait_recv()
    table = jnp.transpose(routes[...])
    chips = lax.broadcasted_iota(jnp.int32, (CHIPS, COLUMN), 0) * PLANES + lax.div(z, 2)
    names_in = (chips + lax.rem(z, 2) * (PLANES // 2)).astype(F32)
    names_out = (chips + c * (PLANES // 2)).astype(F32)
    in_in, in_out = jnp.zeros((CHIPS, COLUMN), F32), jnp.zeros((CHIPS, COLUMN), F32)
    weight = jnp.zeros((CHIPS, COLUMN), F32)
    for k in range(TOPK):
        named = table[k : k + 1]
        in_in = in_in + jnp.where(names_in == named, 1.0, 0.0)
        in_out = in_out + jnp.where(names_out == named, 1.0, 0.0)
        weight = weight + jnp.where(names_out == named, table[TOPK + k : TOPK + k + 1], 0.0)
    member = jnp.concatenate([in_in, in_out], axis=0)
    rank = jnp.dot(member.astype(BF16), mine[0:COLUMN, 0:COLUMN], preferred_element_type=F32)
    rank = jnp.where(member > 0.0, rank, -1.0)
    for d in range(CHIPS):
        pos_in[d] = rank[d : d + 1]
    blank = jnp.zeros((HEAD_SIZE - CHIPS, COLUMN), F32)
    pos_out[...] = jnp.transpose(jnp.concatenate([rank[CHIPS:], blank], axis=0)).astype(BF16)
    share_out[...] = jnp.transpose(jnp.concatenate([weight, blank], axis=0)).astype(BF16)

    ref = heads_in.at[pl.ds(0, PLANES - 1)]
    send(ref, ref, a_s.at[0], a_r.at[0], ctx, z).wait()
    all_of(CHIPS * per, b_s, b_r).wait_send()
    all_of(sum(started), s_s, b_r).wait_send()
    t_all().wait_send()
    t_across(c).wait_send()

    squares = jnp.zeros((TOK, 1), F32)
    for b in range(PLANES):
        summed = resid[:, b * HEADS : (b + 1) * HEADS].astype(F32) + heads_in[b].astype(F32)
        squares = squares + jnp.sum(summed * summed, axis=1, keepdims=True)
    scale = lax.rsqrt(squares / D + 1e-06)

    def summed_at(b):
        at = slice(b * CHUNK, (b + 1) * CHUNK)
        plane, first = b * CHUNK // HEADS, b * CHUNK % HEADS
        return resid[:, at].astype(F32) + heads_in[plane, :, first : first + CHUNK].astype(F32)

    for b in range(2 * CHUNKS):
        normed = summed_at(b) * scale * gain[:, b * CHUNK : (b + 1) * CHUNK]
        gath[b % CHUNKS, z, b // CHUNKS] = normed.astype(BF16)

    def piece(j, r, slot, half):
        some = pl.ds(LAPS[j][0], LAPS[j][1])
        return gath.at[some, slot] if r < 4 else gath.at[some, slot, half]

    def right(j, r):
        ref = piece(j, r, mod8(z - r + 1), 0)
        return send(ref, ref, r_s.at[0], r_r.at[j, r - 1], ctx, mod8(z + 1))

    def left(j, r):
        ref = piece(j, r, mod8(z + r - 1), 1)
        return send(ref, ref, l_s.at[0], l_r.at[j, r - 1], ctx, mod8(z - 1))

    def right_in(j, r):
        ref = piece(j, r, mod8(z - r), 0)
        return send(ref, ref, r_s.at[0], r_r.at[j, r - 1], ctx, mod8(z + 1))

    def left_in(j, r):
        ref = piece(j, r, mod8(z + r), 1)
        return send(ref, ref, l_s.at[0], l_r.at[j, r - 1], ctx, mod8(z - 1))

    def across(k):
        return send(gath.at[k, pl.ds(0, PLANES), 1 - c], toks.at[k, c], c_s.at[0], c_r.at[k], sibling, z)

    def across_in(k):
        ref = toks.at[k, 1 - c]
        return send(ref, ref, c_s.at[0], c_r.at[k], sibling, z)

    def arrived(k):
        across(k).start()
        toks[k, c] = gath[k, :, c]

    lot = pl.ds(0, SLOTS)

    def put(k, row, product):
        for i in range(GRID):
            kv[k * CHIPS + row * GRID + i, lot, :] = product[i * SLOTS : (i + 1) * SLOTS]

    mine_at = pl.ds(pl.multiple_of(chip * SLOTS, SLOTS), SLOTS)

    def d_send(k, d):
        return send(kv.at[k * CHIPS + d, lot, :], rows.at[mine_at, pl.ds(k * CHUNK, CHUNK)], d_s.at[0], d_r.at[x], d * 2 + c, z)

    def dispatch(k):
        across_in(k).wait_recv()

        def step(g):
            xd = lax.rem(x + g, GRID)
            slot = lax.broadcasted_iota(jnp.int32, (SLOTS, COLUMN), 0)
            for i in range(GRID):
                hot[i * SLOTS : (i + 1) * SLOTS, :] = jnp.where(slot.astype(F32) == pos_in[xd * GRID + i], 1.0, 0.0).astype(BF16)
            picked = jnp.dot(hot[...], toks[k].reshape(COLUMN, CHUNK), preferred_element_type=F32)
            put(k, xd, picked.astype(BF16))
            for j in range(1, GRID):
                d_send(k, xd * GRID + lax.rem(y + j, GRID)).start()

            @pl.when(g > 0)
            def _():
                d_send(k, xd * GRID + y).start()

        loop(GRID, step)
        rows[mine_at, k * CHUNK : (k + 1) * CHUNK] = kv[k * CHIPS + chip, lot, :]

    for tick in range(1, len(LAPS) + 5):
        for j, (first_k, count) in enumerate(LAPS):
            r = tick - j
            if 2 <= r <= 5:
                right_in(j, r - 1).wait_recv()
                left_in(j, r - 1).wait_recv()
            if 1 <= r <= 4:
                right(j, r).start()
                left(j, r).start()
            if r == 5:
                for k in range(first_k, first_k + count):
                    arrived(k)
        if tick in RING:
            next_piece(EARLY + RING.index(tick))
        if tick == len(LAPS) + 3:
            for p in range(EARLY + len(RING), PIECES):
                next_piece(p)
        for j, (first_k, count) in enumerate(LAPS):
            if tick - j == (5 if j in (0, len(LAPS) - 1) else 6):
                for k in range(first_k, first_k + count):
                    dispatch(k)

    lane = lax.broadcasted_iota(jnp.int32, (HEAD_SIZE, ROWS), 1)
    owner = lax.broadcasted_iota(jnp.int32, (HEAD_SIZE, ROWS), 0) * SLOTS
    spread = jnp.where((lane >= owner) & (lane < owner + SLOTS), 1.0, 0.0).astype(BF16)

    def build(b):
        at = pl.ds(pl.multiple_of(b * 128, 128), 128)
        slot = jnp.dot(pos_out[at, :], spread, preferred_element_type=F32)
        share = jnp.dot(share_out[at, :], spread, preferred_element_type=F32)
        want = lax.rem(lax.broadcasted_iota(jnp.int32, (128, ROWS), 1), SLOTS).astype(F32)
        comb[at, :] = jnp.where(slot == want, share, 0.0).astype(BF16)

    loop(COLUMN // 128, build)

    pltpu.make_async_copy(wout, wout, w_s.at[1]).wait()

    @pl.when(same)
    def _():
        pltpu.make_async_copy(w_own, win, w_s.at[0]).wait()

    def moved(kind):
        ref = win.at[pl.ds(0, HALF // 2), :]
        return send(ref, ref, x_s.at[kind], x_r.at[kind], ctx, z)

    @pl.when(apart)
    def _():
        moved(0).wait_recv()
        moved(2).wait_recv()

    def span_of(g):
        xs = lax.rem(x - g + GRID, GRID)
        return xs, pl.ds(pl.multiple_of(xs * GROUP, GROUP), GROUP)

    def p_send(g):
        _, at = span_of(g)
        return send(mine.at[at, :], theirs.at[at, :], p_s.at[0], p_r.at[g], sibling, z)

    def first(g):
        xs, at = span_of(g)

        def from_row(count):
            ref = rows.at[pl.ds(0, count), :]
            send(ref, ref, d_s.at[0], d_r.at[xs], ctx, z).wait_recv()

        @pl.when(g == 0)
        def _():
            from_row(GROUP - SLOTS)

        @pl.when(g > 0)
        def _():
            from_row(GROUP)

        mine[at, :] = jnp.dot(rows[at, :], win[...], preferred_element_type=F32).astype(BF16)
        p_send(g).start()

    def h_send(g):
        at = pl.ds(pl.multiple_of(span_of(g)[0] * GROUP, GROUP), GROUP // 2)
        return send(hid_out.at[at, :], hid.at[at, :], h_s.at[0], h_r.at[g], sibling, mate)

    def h_same(g):
        at = pl.ds(pl.multiple_of(span_of(g)[0] * GROUP + GROUP // 2, GROUP // 2), GROUP // 2)
        return send(hid.at[at, :], hid.at[at, :], h_s.at[0], h_r.at[g], ctx, mate)

    def hidden(g):
        p_send(g).wait_recv()
        xs, _ = span_of(g)

        def part(i):
            at = pl.ds(pl.multiple_of(xs * GROUP + i * 32, 32), 32)
            pre = mine[at, :].astype(F32) + theirs[at, :].astype(F32)
            gate, up = pre[:, :FF], pre[:, FF:]
            value = (gate / (1.0 + jnp.exp(-gate)) * up).astype(BF16)

            @pl.when(same)
            def _():
                hid[at, :] = value

            @pl.when(apart)
            def _():
                hid_out[at, :] = value

        loop(GROUP // 32, part)

        @pl.when(apart)
        def _():
            h_send(g).start()

        @pl.when(same)
        def _():
            h_same(g).start()

    def d_all(r_sem):
        ref = kv.at[pl.ds(0, CHUNKS * (CHIPS - 1)), lot, :]
        return send(ref, ref, d_s.at[0], r_sem, ctx, z)

    def o_send(n, d):
        return send(kv.at[n * CHIPS + d, lot, :], back.at[n, mine_at, :], o_s.at[0], o_r.at[n], d * 2 + c, z)

    def second(n, g):
        xs, at = span_of(g)

        @pl.when((n == 0) & apart)
        def _():
            send(hid.at[at, :], hid.at[at, :], h_s.at[0], h_r.at[g], sibling, mate).wait_recv()

        product = jnp.dot(hid[at, :], wout[n], preferred_element_type=F32).astype(BF16)
        put(n, xs, product)
        for j in range(1, GRID):
            o_send(n, xs * GRID + lax.rem(y + j, GRID)).start()

        @pl.when(g > 0)
        def _():
            o_send(n, xs * GRID + y).start()

        @pl.when(g == 0)
        def _():
            back[n, mine_at, :] = kv[n * CHIPS + chip, lot, :]

    def through(g):
        @pl.when(g < GRID)
        def _():
            first(g)

        @pl.when((g > 0) & (g < GRID + 1))
        def _():
            hidden(g - 1)

        @pl.when(g == 2)
        def _():
            d_all(d_r.at[0]).wait_send()

        @pl.when(g > 1)
        def _():
            second(0, g - 2)

    loop(GRID + 2, through)

    units = CHUNKS * 7 // 2 // 4
    for s_sem, r_sem in ((r_s, r_r), (l_s, l_r)):
        ref = gath.at[pl.ds(0, units), pl.ds(0, 4)]
        send(ref, ref, s_sem.at[0], r_sem.at[0, 0], ctx, z).wait_send()
    ref = gath.at[pl.ds(0, CHUNKS // 2)]
    send(ref, ref, c_s.at[0], c_r.at[0], ctx, z).wait_send()

    def u_send(n):
        return send(toks.at[n, 0], sib.at[n], u_s.at[0], u_r.at[n], sibling, z)

    def z_send(n, to):
        return send(gath.at[n, to, 0], parts.at[n, z], z_s.at[0], z_r.at[n], ctx, to)

    def combine(step):
        @pl.when((step > 0) & (step < CHUNKS))
        def _():
            loop(GRID, lambda g: second(step, g))

        @pl.when(step > 1)
        def _():
            n = step - 2

            ref = back.at[n, pl.ds(0, ROWS - SLOTS), :]
            send(ref, ref, o_s.at[0], o_r.at[n], ctx, z).wait_recv()
            total = jnp.dot(comb[tokens_of(1 - c), :], back[n], preferred_element_type=F32)
            toks[n, 0] = total.astype(BF16).reshape(PLANES, TOK, CHUNK)
            u_send(n).start()
            total = jnp.dot(comb[tokens_of(c), :], back[n], preferred_element_type=F32)
            u_send(n).wait_recv()
            total = (total + sib[n].reshape(SPAN, CHUNK).astype(F32)).astype(BF16)
            for s in range(PLANES):
                gath[n, s, 0] = total[s * TOK : (s + 1) * TOK]
            loop(PLANES - 1, lambda r: z_send(n, mod8(z + r + 1)).start())
            parts[n, z] = gath[n, z, 0]

        @pl.when(step > 3)
        def _():
            finish(step - 4)

    def finish(n):
        ref = parts.at[n, pl.ds(0, PLANES - 1)]
        send(ref, ref, z_s.at[0], z_r.at[n], ctx, z).wait_recv()
        for half in range(2):
            total = parts[n, half].astype(F32)
            for q in range(1, PLANES // 2):
                total = total + parts[n, 2 * q + half].astype(F32)
            at = pl.ds(pl.multiple_of((half * CHUNKS + n) * CHUNK, CHUNK), CHUNK)
            per_plane = HEADS // CHUNK
            within = pl.ds(pl.multiple_of(lax.rem(n, per_plane) * CHUNK, CHUNK), CHUNK)
            heads = heads_in[half * (PLANES // 2) + lax.div(n, per_plane), :, within]
            out[:, at] = (resid[:, at].astype(F32) + heads.astype(F32) + total).astype(BF16)

    loop(CHUNKS + 2, combine)
    loop(2, lambda i: finish(CHUNKS - 2 + i))

    send(mine, mine, p_s.at[0], p_r.at[0], ctx, z).wait_send()
    ref = hid.at[pl.ds(0, ROWS // 2), :]
    send(ref, ref, h_s.at[0], h_r.at[0], ctx, z).wait_send()
    ref = kv.at[pl.ds(0, CHUNKS * (CHIPS - 1)), lot, :]
    send(ref, ref, o_s.at[0], o_r.at[0], ctx, z).wait_send()
    ref = toks.at[pl.ds(0, CHUNKS), 0]
    send(ref, ref, u_s.at[0], u_r.at[0], ctx, z).wait_send()
    ref = parts.at[:, pl.ds(0, PLANES - 1)]
    send(ref, ref, z_s.at[0], z_r.at[0], ctx, z).wait_send()

    @pl.when(apart)
    def _():
        moved(0).wait_send()
        moved(1).wait_send()

    @pl.when(same)
    def _():
        moved(2).wait_send()


def run_layer(cols, offsets, own_kv, queries, ids, gates, resid, gain, w_own, w_out):
    vmem = pl.BlockSpec(memory_space=pltpu.VMEM)
    smem = pl.BlockSpec(memory_space=pltpu.SMEM)
    hbm = pl.BlockSpec(memory_space=pl.ANY)
    dma = pltpu.SemaphoreType.DMA
    out, _ = pl.pallas_call(
        layer_kernel,
        out_shape=(
            jax.ShapeDtypeStruct((TOK, D), BF16),
            jax.ShapeDtypeStruct((HALF // 2, 2 * FF), BF16),
        ),
        in_specs=[smem] * 2 + [vmem] * 6 + [hbm] * 2,
        out_specs=(vmem, hbm),
        scratch_shapes=[
            pltpu.VMEM((CHUNKS * CHIPS, BLOCK_TOKENS, CHUNK), BF16),
            pltpu.VMEM((TOK, HEAD_SIZE), F32),
            pltpu.VMEM((COLUMN, HEAD_SIZE), F32),
            pltpu.VMEM((CHIPS, 1, COLUMN), F32),
            pltpu.VMEM((COLUMN, HEAD_SIZE), BF16),
            pltpu.VMEM((COLUMN, HEAD_SIZE), BF16),
            pltpu.VMEM((PLANES, TOK, HEADS), BF16),
            pltpu.VMEM((CHUNKS, PLANES, 2, TOK, CHUNK), BF16),
            pltpu.VMEM((CHUNKS, 2, PLANES, TOK, CHUNK), BF16),
            pltpu.VMEM((GROUP, COLUMN), BF16),
            pltpu.VMEM((ROWS, HALF), BF16),
            pltpu.VMEM((HALF, 2 * FF), BF16),
            pltpu.VMEM((CHUNKS, FF, CHUNK), BF16),
            pltpu.VMEM((ROWS, 2 * FF), BF16),
            pltpu.VMEM((ROWS, 2 * FF), BF16),
            pltpu.VMEM((ROWS, FF), BF16),
            pltpu.VMEM((ROWS, FF), BF16),
            pltpu.VMEM((CHUNKS, ROWS, CHUNK), BF16),
            pltpu.VMEM((COLUMN, ROWS), BF16),
            pltpu.VMEM((CHUNKS, PLANES, TOK, CHUNK), BF16),
            pltpu.VMEM((CHUNKS, PLANES, TOK, CHUNK), BF16),
            dma((1,)), dma((CHIPS, SPAN // BLOCK_TOKENS)),
            dma((1,)), dma((1,)),
            dma((1,)),
            dma((1,)), dma((1,)),
            dma((2,)), dma((2,)),
            dma((1,)), dma((len(LAPS), 4)),
            dma((1,)), dma((len(LAPS), 4)),
            dma((1,)), dma((CHUNKS,)),
            dma((1,)), dma((GRID,)),
            dma((1,)), dma((GRID,)),
            dma((1,)), dma((GRID,)),
            dma((1,)), dma((CHUNKS,)),
            dma((1,)), dma((CHUNKS,)),
            dma((1,)), dma((CHUNKS,)),
            dma((2,)),
            dma((3,)), dma((3,)),
        ],
        compiler_params=pltpu.CompilerParams(
            collective_id=0, has_side_effects=True, vmem_limit_bytes=VMEM_BYTES
        ),
        cost_estimate=pl.CostEstimate(flops=25 * 10**9, bytes_accessed=12 * 10**6, transcendentals=10**6),
        name="layer",
    )(cols, offsets, own_kv, queries, ids, gates, resid, gain, w_own, w_out)
    return out


def local(
    queries, key_value_stack, vertical_cols, slash_offsets, resid,
    norm_gain, expert_ids, gate_weights, w_in, w_out,
):
    z = lax.axis_index("exp")
    heads_dev = queries.shape[1] // HEAD_SIZE
    kv_head = z * heads_dev // (QUERY_HEADS // KEY_VALUE_HEADS)
    own_kv = lax.dynamic_slice_in_dim(key_value_stack, kv_head * HEAD_SIZE, HEAD_SIZE, 2)
    own_kv = own_kv.reshape(-1, BLOCK_TOKENS, 2 * HEAD_SIZE)
    return run_layer(
        vertical_cols.T, slash_offsets.T, own_kv, queries, expert_ids.T, gate_weights.T,
        resid, norm_gain[None, :], w_in[0], w_out[0],
    )


def solution(mesh):
    in_specs = (
        P("ctx", "exp"),
        P("ctx", None, None),
        P(),
        P(),
        P(("ctx", "exp"), None),
        P(),
        P(("ctx", "exp"), None),
        P(("ctx", "exp"), None),
        P(("ctx", "exp"), None, None),
        P(("ctx", "exp"), None, None),
    )
    out_specs = P(("ctx", "exp"), None)
    return jax.shard_map(local, mesh=mesh, in_specs=in_specs, out_specs=out_specs, check_vma=False)
```

```python
import jax
import jax.numpy as jnp
from jax import lax
from jax.experimental import pallas as pl
from jax.experimental.pallas import tpu as pltpu
from jax.sharding import PartitionSpec as P

D = 4096
QUERY_HEADS = 32
KEY_VALUE_HEADS = 4
HEAD_SIZE = 128
FF = 768
TOPK = 8
BLOCK_TOKENS = 128
NV = 4
NS = 2
WINDOW = NS + NV

GRID = 4
CHIPS = GRID * GRID
PLANES = 8
TOK = 64
SPAN = PLANES * TOK
COLUMN = 2 * SPAN
CAP = 5
SLOTS = CAP * 2 * PLANES
GROUP = GRID * SLOTS
ROWS = CHIPS * SLOTS
HALF = D // 2
CHUNKS = 8
CHUNK = HALF // CHUNKS
HEADS = D // PLANES
PIECES = 16
PIECE = HALF // 2 // PIECES
EARLY = 5
RING = (5, 6, 7, 8, 9, 10, 11)
LAPS = tuple((k, 1) for k in range(CHUNKS))
VMEM_BYTES = 63 * 2**20
MESH = pl.DeviceIdType.MESH
BF16 = jnp.bfloat16
F32 = jnp.float32


def attend(q, kv, seen_blocks):
    heads = q.shape[1] // HEAD_SIZE
    q = jnp.concatenate([q[:, h * HEAD_SIZE : (h + 1) * HEAD_SIZE] for h in range(heads)], axis=0)
    keys = jnp.concatenate([block[:, :HEAD_SIZE] for block in kv], axis=0)
    values = jnp.concatenate([block[:, HEAD_SIZE:] for block in kv], axis=0)
    scores = lax.dot_general(q, keys, (((1,), (1,)), ((), ())), preferred_element_type=F32)
    scores = scores * HEAD_SIZE ** (-0.5)
    row = lax.broadcasted_iota(jnp.int32, (heads * BLOCK_TOKENS, BLOCK_TOKENS), 0) % BLOCK_TOKENS
    col = lax.broadcasted_iota(jnp.int32, (heads * BLOCK_TOKENS, BLOCK_TOKENS), 1)
    parts, masks = [], []
    for j in range(WINDOW):
        part = scores[:, j * BLOCK_TOKENS : (j + 1) * BLOCK_TOKENS]
        seen = jnp.full(part.shape, seen_blocks[j], jnp.int32) > 0
        if j == 0:
            seen = seen & (col <= row)
        parts.append(jnp.where(seen, part, -1e30))
        masks.append(seen)
    top = parts[0]
    for part in parts[1:]:
        top = jnp.maximum(top, part)
    top = jnp.max(top, axis=1, keepdims=True)
    parts = [jnp.where(seen, jnp.exp(part - top), 0.0) for part, seen in zip(parts, masks)]
    total = parts[0]
    for part in parts[1:]:
        total = total + part
    total = jnp.sum(total, axis=1, keepdims=True)
    probs = jnp.concatenate([(part / total).astype(BF16) for part in parts], axis=1)
    result = jnp.dot(probs, values, preferred_element_type=F32).astype(BF16)
    return jnp.concatenate([result[h * BLOCK_TOKENS : (h + 1) * BLOCK_TOKENS] for h in range(heads)], axis=1)


def layer_kernel(
    cols, offsets, own, queries, ids, gates, resid, gain, w_own, w_out, out, w_stage,
    kv, route, routes, pos_in, pos_out, share_out, heads_in, gath, toks, hot, rows, win, wout,
    mine, theirs, hid_out, hid, back, comb, sib, parts,
    s_s, s_r, b_s, b_r, o_c, a_s, a_r, t_s, t_r,
    r_s, r_r, l_s, l_r, c_s, c_r, d_s, d_r, p_s, p_r, h_s, h_r, o_s, o_r, u_s, u_r, z_s, z_r, w_s, x_s, x_r,
):
    ctx = lax.axis_index("ctx")
    z = lax.axis_index("exp")
    chip, c = lax.div(ctx, 2), lax.rem(ctx, 2)
    x, y = lax.div(chip, GRID), lax.rem(chip, GRID)
    sibling = chip * 2 + 1 - c
    mate = lax.div(z, 2) * 2 + 1 - lax.rem(z, 2)
    same = c == lax.rem(z, 2)
    apart = c != lax.rem(z, 2)

    def send(src, dst, s_sem, r_sem, to_ctx, to_z):
        return pltpu.make_async_remote_copy(
            src_ref=src, dst_ref=dst, send_sem=s_sem, recv_sem=r_sem,
            device_id=(to_ctx, to_z), device_id_type=MESH,
        )

    def loop(count, body):
        lax.fori_loop(0, count, lambda i, carry: (body(i), carry)[1], 0)

    def mod8(v):
        return lax.rem(v + 2 * PLANES, PLANES)

    barrier = pltpu.get_barrier_semaphore()

    def greet(cx, zz):
        pl.semaphore_signal(barrier, inc=1, device_id=(cx, zz), device_id_type=MESH)

    def greet_chip(d):
        @pl.when(d != chip)
        def _():
            greet(d * 2 + c, z)

    loop(CHIPS, greet_chip)
    loop(PLANES - 1, lambda r: greet(ctx, mod8(z + r + 1)))
    greet(sibling, z)
    greet(sibling, mate)

    def wout_copy(k):
        return pltpu.make_async_copy(w_out.at[:, pl.ds(k * CHUNK, CHUNK)], wout.at[k], w_s.at[1])

    def piece_rows(first, p):
        return pl.ds(pl.multiple_of(first + p * PIECE, PIECE), PIECE)

    def straight(p):
        at = piece_rows(0, p)
        return send(w_own.at[at, :], win.at[at, :], x_s.at[0], x_r.at[0], sibling, mate)

    def to_stage():
        return send(w_own.at[pl.ds(HALF // 2, HALF // 2), :], w_stage, x_s.at[1], x_r.at[1], sibling, z)

    def from_stage(p):
        src, dst = piece_rows(0, p), piece_rows(HALF // 2, p)
        return send(w_stage.at[src, :], win.at[dst, :], x_s.at[2], x_r.at[2], ctx, mate)

    def next_piece(p):
        @pl.when(apart)
        def _():
            straight(p).start()

        @pl.when(same)
        def _():
            from_stage(p).start()

    @pl.when(same)
    def _():
        pltpu.make_async_copy(w_own, win, w_s.at[0]).start()

    for k in range(CHUNKS):
        wout_copy(k).start()

    def above(b):
        at = pl.ds(pl.multiple_of(b * 128, 128), 128)
        row = lax.broadcasted_iota(jnp.int32, (128, COLUMN), 0) + b * 128
        col = lax.broadcasted_iota(jnp.int32, (128, COLUMN), 1)
        mine[at, 0:COLUMN] = jnp.where(row < col, 1.0, 0.0).astype(BF16)

    loop(COLUMN // 128, above)

    def tokens_of(core):
        return pl.ds(pl.multiple_of(core * SPAN, SPAN), SPAN)

    def place(core, slot):
        return pl.ds(pl.multiple_of(core * SPAN + slot * TOK, TOK), TOK)

    shares = gates[...] / jnp.sum(gates[...], axis=0, keepdims=True)
    blank = jnp.zeros((HEAD_SIZE - 2 * TOPK, TOK), F32)
    both = jnp.concatenate([ids[...].astype(F32), shares, blank], axis=0)
    both = jnp.concatenate([both, jnp.zeros((HEAD_SIZE, HEAD_SIZE - TOK), F32)], axis=1)
    route[...] = jnp.transpose(both)[:TOK]
    routes[place(c, z), :] = route[...]

    def t_send(to):
        return send(route, routes.at[place(c, z), :], t_s.at[0], t_r.at[0], ctx, to)

    def t_all():
        ref = routes.at[pl.ds(0, (PLANES - 1) * TOK), :]
        return send(ref, ref, t_s.at[0], t_r.at[0], ctx, z)

    def t_across(core):
        at = tokens_of(core)
        return send(routes.at[at, :], routes.at[at, :], t_s.at[1], t_r.at[1], sibling, z)

    spot = (x, y)

    def chip_at(half, du, dv):
        u, v = spot[half], spot[1 - half]
        u, v = lax.rem(u + du + GRID, GRID), lax.rem(v + dv + GRID, GRID)
        return u * GRID + v if half == 0 else v * GRID + u

    pl.semaphore_wait(barrier, (CHIPS - 1) + (PLANES - 1) + 2)

    per = SPAN // BLOCK_TOKENS
    started = []

    def blocks_at(first, count):
        return kv.at[pl.ds(first, count)]

    def own_at(first, count):
        return own.at[pl.ds(first, count)]

    def launch(src, half, blocks, first, at, du, dv):
        to = chip_at(half, du, dv) * 2 + c
        dst = blocks_at((at * 2 + c) * per + first, blocks)
        send(src, dst, s_s.at[0], s_r.at[at, first], to, z).start()
        started.append(blocks)

    def held(at, first, blocks):
        return blocks_at((at * 2 + c) * per + first, blocks)

    def arrive(at, first, blocks):
        ref = held(at, first, blocks)
        send(ref, ref, s_s.at[0], s_r.at[at, first], ctx, z).wait_recv()

    def share(src, at, half):
        dst = blocks_at((at * 2 + c) * per + 2 * half, 2)
        send(src, dst, b_s.at[0], b_r.at[0], sibling, z).start()

    for half in range(2):
        for du in (1, -1):
            launch(own_at(2 * half, 2), half, 2, 2 * half, chip, du, 0)
    for half in range(2):
        for dv in (1, -1):
            launch(own_at(2 * half, 2), half, 2, 2 * half, chip, 0, dv)
    for half in range(2):
        share(own_at(2 * half, 2), chip, half)
    own_copy = pltpu.make_async_copy(own, blocks_at(ctx * per, per), o_c.at[0])
    own_copy.start()
    loop(PLANES - 1, lambda r: t_send(mod8(z + r + 1)).start())

    @pl.when(apart)
    def _():
        to_stage().start()
        loop(EARLY, lambda p: straight(p).start())

    def onward(half, du):
        at = chip_at(half, du, 0)
        for dv in (1, -1):
            launch(held(at, 2 * half, 2), half, 2, 2 * half, at, 0, dv)
        share(held(at, 2 * half, 2), at, half)

    for half in range(2):
        before, after = chip_at(half, -1, 0), chip_at(half, 1, 0)
        arrive(before, 2 * half, 2)
        launch(held(before, 2 * half, 1), half, 1, 2 * half, before, 1, 0)
        arrive(after, 2 * half, 2)
        launch(held(after, 2 * half + 1, 1), half, 1, 2 * half + 1, after, -1, 0)

    @pl.when(same)
    def _():
        to_stage().wait_recv()
        loop(EARLY, lambda p: from_stage(p).start())

    for half in range(2):
        onward(half, -1)
        onward(half, 1)
    t_all().wait_recv()
    t_across(c).start()
    for half in range(2):
        far = chip_at(half, 2, 0)
        arrive(far, 2 * half, 1)
        arrive(far, 2 * half + 1, 1)
        onward(half, 2)
    for du in (0, -1, 1, 2):
        for half in range(2):
            before, after = chip_at(half, du, -1), chip_at(half, du, 1)
            arrive(before, 2 * half, 2)
            launch(held(before, 2 * half, 1), half, 1, 2 * half, before, 0, 1)
            arrive(after, 2 * half, 2)
            launch(held(after, 2 * half + 1, 1), half, 1, 2 * half + 1, after, 0, -1)
            share(held(before, 2 * half, 2), before, half)
            share(held(after, 2 * half, 2), after, half)
    for du in (0, -1, 1, 2):
        for half in range(2):
            far = chip_at(half, du, 2)
            arrive(far, 2 * half, 1)
            arrive(far, 2 * half + 1, 1)
            share(held(far, 2 * half, 2), far, half)

    def all_of(blocks, s_sem, r_sem):
        ref = blocks_at(0, blocks)
        return send(ref, ref, s_sem.at[0], r_sem.at[0], sibling, z)

    all_of(CHIPS * per, b_s, b_r).wait_recv()
    own_copy.wait()

    def a_send(to):
        at = pl.ds(pl.multiple_of(to * TOK, TOK), TOK)
        return send(comb.at[at, pl.ds(0, HEADS)], heads_in.at[z], a_s.at[0], a_r.at[0], ctx, to)

    def block(turn, carry):
        i = lax.rem(turn + lax.div(z, 2) + 1, SPAN // BLOCK_TOKENS)
        at = pl.ds(pl.multiple_of(i * BLOCK_TOKENS, BLOCK_TOKENS), BLOCK_TOKENS)
        number = ctx * per + i
        slash = [number - offsets[j, number] for j in range(NS)]
        column = [cols[j, number] for j in range(NV)]
        kept = [v >= 0 for v in slash]
        for j in range(NV):
            keep = column[j] >= 0
            for other in slash + column[:j]:
                keep = jnp.logical_and(keep, column[j] != other)
            kept.append(keep)
        chosen = [kv[jnp.maximum(v, 0)] for v in slash + column]
        kept = [jnp.where(v, 1, 0) for v in kept]
        comb[at, 0:HEADS] = attend(queries[at, :], chosen, kept)
        for part in range(BLOCK_TOKENS // TOK):
            to = i * (BLOCK_TOKENS // TOK) + part

            @pl.when(to != z)
            def _():
                a_send(to).start()

        return carry

    lax.fori_loop(0, SPAN // BLOCK_TOKENS, block, 0)
    heads_in[z] = comb[pl.ds(pl.multiple_of(z * TOK, TOK), TOK), 0:HEADS]

    t_across(1 - c).wait_recv()
    table = jnp.transpose(routes[...])
    chips = lax.broadcasted_iota(jnp.int32, (CHIPS, COLUMN), 0) * PLANES + lax.div(z, 2)
    names_in = (chips + lax.rem(z, 2) * (PLANES // 2)).astype(F32)
    names_out = (chips + c * (PLANES // 2)).astype(F32)
    in_in, in_out = jnp.zeros((CHIPS, COLUMN), F32), jnp.zeros((CHIPS, COLUMN), F32)
    weight = jnp.zeros((CHIPS, COLUMN), F32)
    for k in range(TOPK):
        named = table[k : k + 1]
        in_in = in_in + jnp.where(names_in == named, 1.0, 0.0)
        in_out = in_out + jnp.where(names_out == named, 1.0, 0.0)
        weight = weight + jnp.where(names_out == named, table[TOPK + k : TOPK + k + 1], 0.0)
    member = jnp.concatenate([in_in, in_out], axis=0)
    rank = jnp.dot(member.astype(BF16), mine[0:COLUMN, 0:COLUMN], preferred_element_type=F32)
    rank = jnp.where(member > 0.0, rank, -1.0)
    for d in range(CHIPS):
        pos_in[d] = rank[d : d + 1]
    blank = jnp.zeros((HEAD_SIZE - CHIPS, COLUMN), F32)
    pos_out[...] = jnp.transpose(jnp.concatenate([rank[CHIPS:], blank], axis=0)).astype(BF16)
    share_out[...] = jnp.transpose(jnp.concatenate([weight, blank], axis=0)).astype(BF16)

    ref = heads_in.at[pl.ds(0, PLANES - 1)]
    send(ref, ref, a_s.at[0], a_r.at[0], ctx, z).wait()
    all_of(CHIPS * per, b_s, b_r).wait_send()
    all_of(sum(started), s_s, b_r).wait_send()
    t_all().wait_send()
    t_across(c).wait_send()

    squares = jnp.zeros((TOK, 1), F32)
    for b in range(PLANES):
        summed = resid[:, b * HEADS : (b + 1) * HEADS].astype(F32) + heads_in[b].astype(F32)
        squares = squares + jnp.sum(summed * summed, axis=1, keepdims=True)
    scale = lax.rsqrt(squares / D + 1e-06)

    def summed_at(b):
        at = slice(b * CHUNK, (b + 1) * CHUNK)
        plane, first = b * CHUNK // HEADS, b * CHUNK % HEADS
        return resid[:, at].astype(F32) + heads_in[plane, :, first : first + CHUNK].astype(F32)

    for b in range(2 * CHUNKS):
        normed = summed_at(b) * scale * gain[:, b * CHUNK : (b + 1) * CHUNK]
        gath[b % CHUNKS, z, b // CHUNKS] = normed.astype(BF16)

    def piece(j, r, slot, half):
        some = pl.ds(LAPS[j][0], LAPS[j][1])
        return gath.at[some, slot] if r < 4 else gath.at[some, slot, half]

    def right(j, r):
        ref = piece(j, r, mod8(z - r + 1), 0)
        return send(ref, ref, r_s.at[0], r_r.at[j, r - 1], ctx, mod8(z + 1))

    def left(j, r):
        ref = piece(j, r, mod8(z + r - 1), 1)
        return send(ref, ref, l_s.at[0], l_r.at[j, r - 1], ctx, mod8(z - 1))

    def right_in(j, r):
        ref = piece(j, r, mod8(z - r), 0)
        return send(ref, ref, r_s.at[0], r_r.at[j, r - 1], ctx, mod8(z + 1))

    def left_in(j, r):
        ref = piece(j, r, mod8(z + r), 1)
        return send(ref, ref, l_s.at[0], l_r.at[j, r - 1], ctx, mod8(z - 1))

    def across(k):
        return send(gath.at[k, pl.ds(0, PLANES), 1 - c], toks.at[k, c], c_s.at[0], c_r.at[k], sibling, z)

    def across_in(k):
        ref = toks.at[k, 1 - c]
        return send(ref, ref, c_s.at[0], c_r.at[k], sibling, z)

    def arrived(k):
        across(k).start()
        toks[k, c] = gath[k, :, c]

    lot = pl.ds(0, SLOTS)

    def put(k, row, product):
        for i in range(GRID):
            kv[k * CHIPS + row * GRID + i, lot, :] = product[i * SLOTS : (i + 1) * SLOTS]

    mine_at = pl.ds(pl.multiple_of(chip * SLOTS, SLOTS), SLOTS)

    def d_send(k, d):
        return send(kv.at[k * CHIPS + d, lot, :], rows.at[mine_at, pl.ds(k * CHUNK, CHUNK)], d_s.at[0], d_r.at[x], d * 2 + c, z)

    def dispatch(k):
        across_in(k).wait_recv()

        def step(g):
            xd = lax.rem(x + g, GRID)
            slot = lax.broadcasted_iota(jnp.int32, (SLOTS, COLUMN), 0)
            for i in range(GRID):
                hot[i * SLOTS : (i + 1) * SLOTS, :] = jnp.where(slot.astype(F32) == pos_in[xd * GRID + i], 1.0, 0.0).astype(BF16)
            picked = jnp.dot(hot[...], toks[k].reshape(COLUMN, CHUNK), preferred_element_type=F32)
            put(k, xd, picked.astype(BF16))
            for j in range(1, GRID):
                d_send(k, xd * GRID + lax.rem(y + j, GRID)).start()

            @pl.when(g > 0)
            def _():
                d_send(k, xd * GRID + y).start()

        loop(GRID, step)
        rows[mine_at, k * CHUNK : (k + 1) * CHUNK] = kv[k * CHIPS + chip, lot, :]

    for tick in range(1, len(LAPS) + 5):
        for j, (first_k, count) in enumerate(LAPS):
            r = tick - j
            if 2 <= r <= 5:
                right_in(j, r - 1).wait_recv()
                left_in(j, r - 1).wait_recv()
            if 1 <= r <= 4:
                right(j, r).start()
                left(j, r).start()
            if r == 5:
                for k in range(first_k, first_k + count):
                    arrived(k)
        if tick in RING:
            next_piece(EARLY + RING.index(tick))
        if tick == len(LAPS) + 3:
            for p in range(EARLY + len(RING), PIECES):
                next_piece(p)
        for j, (first_k, count) in enumerate(LAPS):
            if tick - j == (5 if j in (0, len(LAPS) - 1) else 6):
                for k in range(first_k, first_k + count):
                    dispatch(k)

    lane = lax.broadcasted_iota(jnp.int32, (HEAD_SIZE, ROWS), 1)
    owner = lax.broadcasted_iota(jnp.int32, (HEAD_SIZE, ROWS), 0) * SLOTS
    spread = jnp.where((lane >= owner) & (lane < owner + SLOTS), 1.0, 0.0).astype(BF16)

    def build(b):
        at = pl.ds(pl.multiple_of(b * 128, 128), 128)
        slot = jnp.dot(pos_out[at, :], spread, preferred_element_type=F32)
        share = jnp.dot(share_out[at, :], spread, preferred_element_type=F32)
        want = lax.rem(lax.broadcasted_iota(jnp.int32, (128, ROWS), 1), SLOTS).astype(F32)
        comb[at, :] = jnp.where(slot == want, share, 0.0).astype(BF16)

    loop(COLUMN // 128, build)

    pltpu.make_async_copy(wout, wout, w_s.at[1]).wait()

    @pl.when(same)
    def _():
        pltpu.make_async_copy(w_own, win, w_s.at[0]).wait()

    def moved(kind):
        ref = win.at[pl.ds(0, HALF // 2), :]
        return send(ref, ref, x_s.at[kind], x_r.at[kind], ctx, z)

    @pl.when(apart)
    def _():
        moved(0).wait_recv()
        moved(2).wait_recv()

    def span_of(g):
        xs = lax.rem(x - g + GRID, GRID)
        return xs, pl.ds(pl.multiple_of(xs * GROUP, GROUP), GROUP)

    def p_send(g):
        _, at = span_of(g)
        return send(mine.at[at, :], theirs.at[at, :], p_s.at[0], p_r.at[g], sibling, z)

    def first(g):
        xs, at = span_of(g)

        def from_row(count):
            ref = rows.at[pl.ds(0, count), :]
            send(ref, ref, d_s.at[0], d_r.at[xs], ctx, z).wait_recv()

        @pl.when(g == 0)
        def _():
            from_row(GROUP - SLOTS)

        @pl.when(g > 0)
        def _():
            from_row(GROUP)

        mine[at, :] = jnp.dot(rows[at, :], win[...], preferred_element_type=F32).astype(BF16)
        p_send(g).start()

    def h_send(g):
        at = pl.ds(pl.multiple_of(span_of(g)[0] * GROUP, GROUP), GROUP // 2)
        return send(hid_out.at[at, :], hid.at[at, :], h_s.at[0], h_r.at[g], sibling, mate)

    def h_same(g):
        at = pl.ds(pl.multiple_of(span_of(g)[0] * GROUP + GROUP // 2, GROUP // 2), GROUP // 2)
        return send(hid.at[at, :], hid.at[at, :], h_s.at[0], h_r.at[g], ctx, mate)

    def hidden(g):
        p_send(g).wait_recv()
        xs, _ = span_of(g)

        def part(i):
            at = pl.ds(pl.multiple_of(xs * GROUP + i * 32, 32), 32)
            pre = mine[at, :].astype(F32) + theirs[at, :].astype(F32)
            gate, up = pre[:, :FF], pre[:, FF:]
            value = (gate / (1.0 + jnp.exp(-gate)) * up).astype(BF16)

            @pl.when(same)
            def _():
                hid[at, :] = value

            @pl.when(apart)
            def _():
                hid_out[at, :] = value

        loop(GROUP // 32, part)

        @pl.when(apart)
        def _():
            h_send(g).start()

        @pl.when(same)
        def _():
            h_same(g).start()

    def d_all(r_sem):
        ref = kv.at[pl.ds(0, CHUNKS * (CHIPS - 1)), lot, :]
        return send(ref, ref, d_s.at[0], r_sem, ctx, z)

    def o_send(n, d):
        return send(kv.at[n * CHIPS + d, lot, :], back.at[n, mine_at, :], o_s.at[0], o_r.at[n], d * 2 + c, z)

    def second(n, g):
        xs, at = span_of(g)

        @pl.when((n == 0) & apart)
        def _():
            send(hid.at[at, :], hid.at[at, :], h_s.at[0], h_r.at[g], sibling, mate).wait_recv()

        product = jnp.dot(hid[at, :], wout[n], preferred_element_type=F32).astype(BF16)
        put(n, xs, product)
        for j in range(1, GRID):
            o_send(n, xs * GRID + lax.rem(y + j, GRID)).start()

        @pl.when(g > 0)
        def _():
            o_send(n, xs * GRID + y).start()

        @pl.when(g == 0)
        def _():
            back[n, mine_at, :] = kv[n * CHIPS + chip, lot, :]

    def through(g):
        @pl.when(g < GRID)
        def _():
            first(g)

        @pl.when((g > 0) & (g < GRID + 1))
        def _():
            hidden(g - 1)

        @pl.when(g == 2)
        def _():
            d_all(d_r.at[0]).wait_send()

        @pl.when(g > 1)
        def _():
            second(0, g - 2)

    loop(GRID + 2, through)

    units = CHUNKS * 7 // 2 // 4
    for s_sem, r_sem in ((r_s, r_r), (l_s, l_r)):
        ref = gath.at[pl.ds(0, units), pl.ds(0, 4)]
        send(ref, ref, s_sem.at[0], r_sem.at[0, 0], ctx, z).wait_send()
    ref = gath.at[pl.ds(0, CHUNKS // 2)]
    send(ref, ref, c_s.at[0], c_r.at[0], ctx, z).wait_send()

    def u_send(n):
        return send(toks.at[n, 0], sib.at[n], u_s.at[0], u_r.at[n], sibling, z)

    def z_send(n, to):
        return send(gath.at[n, to, 0], parts.at[n, z], z_s.at[0], z_r.at[n], ctx, to)

    def combine(step):
        @pl.when((step > 0) & (step < CHUNKS))
        def _():
            loop(GRID, lambda g: second(step, g))

        @pl.when(step > 2)
        def _():
            n = step - 3

            ref = back.at[n, pl.ds(0, ROWS - SLOTS), :]
            send(ref, ref, o_s.at[0], o_r.at[n], ctx, z).wait_recv()
            total = jnp.dot(comb[tokens_of(1 - c), :], back[n], preferred_element_type=F32)
            toks[n, 0] = total.astype(BF16).reshape(PLANES, TOK, CHUNK)
            u_send(n).start()
            total = jnp.dot(comb[tokens_of(c), :], back[n], preferred_element_type=F32)
            u_send(n).wait_recv()
            total = (total + sib[n].reshape(SPAN, CHUNK).astype(F32)).astype(BF16)
            for s in range(PLANES):
                gath[n, s, 0] = total[s * TOK : (s + 1) * TOK]
            loop(PLANES - 1, lambda r: z_send(n, mod8(z + r + 1)).start())
            parts[n, z] = gath[n, z, 0]

        @pl.when(step > 4)
        def _():
            finish(step - 5)

    def finish(n):
        ref = parts.at[n, pl.ds(0, PLANES - 1)]
        send(ref, ref, z_s.at[0], z_r.at[n], ctx, z).wait_recv()
        for half in range(2):
            total = parts[n, half].astype(F32)
            for q in range(1, PLANES // 2):
                total = total + parts[n, 2 * q + half].astype(F32)
            at = pl.ds(pl.multiple_of((half * CHUNKS + n) * CHUNK, CHUNK), CHUNK)
            per_plane = HEADS // CHUNK
            within = pl.ds(pl.multiple_of(lax.rem(n, per_plane) * CHUNK, CHUNK), CHUNK)
            heads = heads_in[half * (PLANES // 2) + lax.div(n, per_plane), :, within]
            out[:, at] = (resid[:, at].astype(F32) + heads.astype(F32) + total).astype(BF16)

    loop(CHUNKS + 3, combine)
    loop(2, lambda i: finish(CHUNKS - 2 + i))

    send(mine, mine, p_s.at[0], p_r.at[0], ctx, z).wait_send()
    ref = hid.at[pl.ds(0, ROWS // 2), :]
    send(ref, ref, h_s.at[0], h_r.at[0], ctx, z).wait_send()
    ref = kv.at[pl.ds(0, CHUNKS * (CHIPS - 1)), lot, :]
    send(ref, ref, o_s.at[0], o_r.at[0], ctx, z).wait_send()
    ref = toks.at[pl.ds(0, CHUNKS), 0]
    send(ref, ref, u_s.at[0], u_r.at[0], ctx, z).wait_send()
    ref = parts.at[:, pl.ds(0, PLANES - 1)]
    send(ref, ref, z_s.at[0], z_r.at[0], ctx, z).wait_send()

    @pl.when(apart)
    def _():
        moved(0).wait_send()
        moved(1).wait_send()

    @pl.when(same)
    def _():
        moved(2).wait_send()


def run_layer(cols, offsets, own_kv, queries, ids, gates, resid, gain, w_own, w_out):
    vmem = pl.BlockSpec(memory_space=pltpu.VMEM)
    smem = pl.BlockSpec(memory_space=pltpu.SMEM)
    hbm = pl.BlockSpec(memory_space=pl.ANY)
    dma = pltpu.SemaphoreType.DMA
    out, _ = pl.pallas_call(
        layer_kernel,
        out_shape=(
            jax.ShapeDtypeStruct((TOK, D), BF16),
            jax.ShapeDtypeStruct((HALF // 2, 2 * FF), BF16),
        ),
        in_specs=[smem] * 2 + [vmem] * 6 + [hbm] * 2,
        out_specs=(vmem, hbm),
        scratch_shapes=[
            pltpu.VMEM((CHUNKS * CHIPS, BLOCK_TOKENS, CHUNK), BF16),
            pltpu.VMEM((TOK, HEAD_SIZE), F32),
            pltpu.VMEM((COLUMN, HEAD_SIZE), F32),
            pltpu.VMEM((CHIPS, 1, COLUMN), F32),
            pltpu.VMEM((COLUMN, HEAD_SIZE), BF16),
            pltpu.VMEM((COLUMN, HEAD_SIZE), BF16),
            pltpu.VMEM((PLANES, TOK, HEADS), BF16),
            pltpu.VMEM((CHUNKS, PLANES, 2, TOK, CHUNK), BF16),
            pltpu.VMEM((CHUNKS, 2, PLANES, TOK, CHUNK), BF16),
            pltpu.VMEM((GROUP, COLUMN), BF16),
            pltpu.VMEM((ROWS, HALF), BF16),
            pltpu.VMEM((HALF, 2 * FF), BF16),
            pltpu.VMEM((CHUNKS, FF, CHUNK), BF16),
            pltpu.VMEM((ROWS, 2 * FF), BF16),
            pltpu.VMEM((ROWS, 2 * FF), BF16),
            pltpu.VMEM((ROWS, FF), BF16),
            pltpu.VMEM((ROWS, FF), BF16),
            pltpu.VMEM((CHUNKS, ROWS, CHUNK), BF16),
            pltpu.VMEM((COLUMN, ROWS), BF16),
            pltpu.VMEM((CHUNKS, PLANES, TOK, CHUNK), BF16),
            pltpu.VMEM((CHUNKS, PLANES, TOK, CHUNK), BF16),
            dma((1,)), dma((CHIPS, SPAN // BLOCK_TOKENS)),
            dma((1,)), dma((1,)),
            dma((1,)),
            dma((1,)), dma((1,)),
            dma((2,)), dma((2,)),
            dma((1,)), dma((len(LAPS), 4)),
            dma((1,)), dma((len(LAPS), 4)),
            dma((1,)), dma((CHUNKS,)),
            dma((1,)), dma((GRID,)),
            dma((1,)), dma((GRID,)),
            dma((1,)), dma((GRID,)),
            dma((1,)), dma((CHUNKS,)),
            dma((1,)), dma((CHUNKS,)),
            dma((1,)), dma((CHUNKS,)),
            dma((2,)),
            dma((3,)), dma((3,)),
        ],
        compiler_params=pltpu.CompilerParams(
            collective_id=0, has_side_effects=True, vmem_limit_bytes=VMEM_BYTES
        ),
        cost_estimate=pl.CostEstimate(flops=25 * 10**9, bytes_accessed=12 * 10**6, transcendentals=10**6),
        name="layer",
    )(cols, offsets, own_kv, queries, ids, gates, resid, gain, w_own, w_out)
    return out


def local(
    queries, key_value_stack, vertical_cols, slash_offsets, resid,
    norm_gain, expert_ids, gate_weights, w_in, w_out,
):
    z = lax.axis_index("exp")
    heads_dev = queries.shape[1] // HEAD_SIZE
    kv_head = z * heads_dev // (QUERY_HEADS // KEY_VALUE_HEADS)
    own_kv = lax.dynamic_slice_in_dim(key_value_stack, kv_head * HEAD_SIZE, HEAD_SIZE, 2)
    own_kv = own_kv.reshape(-1, BLOCK_TOKENS, 2 * HEAD_SIZE)
    return run_layer(
        vertical_cols.T, slash_offsets.T, own_kv, queries, expert_ids.T, gate_weights.T,
        resid, norm_gain[None, :], w_in[0], w_out[0],
    )


def solution(mesh):
    in_specs = (
        P("ctx", "exp"),
        P("ctx", None, None),
        P(),
        P(),
        P(("ctx", "exp"), None),
        P(),
        P(("ctx", "exp"), None),
        P(("ctx", "exp"), None),
        P(("ctx", "exp"), None, None),
        P(("ctx", "exp"), None, None),
    )
    out_specs = P(("ctx", "exp"), None)
    return jax.shard_map(local, mesh=mesh, in_specs=in_specs, out_specs=out_specs, check_vma=False)
```
